32 devices in a mesh: cuts: 2 (over x), row: 16 (over z, y, core).
Axes of the slice: x: 2, y: 2, z: 4, core: 2. Of those that a mesh axis runs over, the one named last changes fastest.
Arguments:
- left_stem: bfloat16 [2, 8192, 4096], P(None, ('cuts', 'row')), parts along dimension 1, may hold values from -6 to 6
- right_stem: bfloat16 [2, 1024, 4096], P(None, ('cuts', 'row')), parts along dimension 1, may hold values from -6 to 6
- branches: bfloat16 [10, 2, 2, 512, 512], P(None, None, None, 'row'), may hold values from -0.1875 to 0.1875
- slice_bits: int32 [20], P('cuts'), parts along dimension 0, may hold values from 0 to 1
- perms: int32 [10, 8], P('cuts'), parts along dimension 0, may hold values from 0 to 7, each once within a row
Outputs:
- amplitude: float32 [2, 8192, 512], P(None, ('cuts', 'row')), parts along dimension 1
The draws below stay inside these ranges and needn't reach their ends.
There are 2 independent parts, one for each index of `cuts`. The reference program is written for one: setup_inputs(seed, part) draws one part's arguments, and reference() takes and returns one part's arrays. A program takes and returns all parts, laid end to end along the dimension named above; an argument that names none is the same for every part. Nothing has to cross between parts.
Inputs may be any that keep to these rules, and one draw needn't show every extreme that they name: `perms`: each row holds every group number once.
All inputs are finite; a program needn't handle non-finite values.
Results may differ from the reference program's by a relative error of at most 0.012.
Values may be sent and summed in bfloat16 or wider, within the bound.
A program may use at most 64 MiB of HBM per device.

```python
import math
import jax
import jax.numpy as jnp

BR = 512
NBLK = 8
LROWS = 4096
RROWS = 512
LSWEEPS = 3
RSWEEPS = 2
COLS = 4096
NBR = 10


def place_ends(drawn, stream_key, least, top_value):
    shape = drawn.shape
    spot = [jax.random.randint(jax.random.fold_in(stream_key, axis), (), 0, shape[axis]) for axis in range(len(shape))]
    drawn = drawn.at[tuple(spot)].set(least)
    longest = shape.index(max(shape))
    spot[longest] = (spot[longest] + 1) % shape[longest]
    return drawn.at[tuple(spot)].set(top_value)


def block_scale(key, shape, split, low, high):
    loudness, own = 1.0, jax.random.fold_in(key, 6)
    for axis_at, parts in split:
        steps = jnp.exp(jax.random.uniform(jax.random.fold_in(own, axis_at), (parts,), jnp.float32, low / len(split), high / len(split)))
        loudness = loudness * jnp.repeat(steps, shape[axis_at] // parts).reshape([-1 if axis == axis_at else 1 for axis in range(len(shape))])
    return loudness


def scatter_about(key, shape, deviation, limit, cuts=(), kind=jnp.bfloat16):
    array = jax.random.normal(key, shape, jnp.float32) * deviation
    if len(cuts) > 0:
        array = block_scale(key, shape, cuts, -0.22, 0.18) * array
    return jnp.clip(array, min=-limit, max=limit).astype(kind)


def setup_inputs(seed: int = 0, part: int = 0) -> dict:
    streams_of = jax.random.split(jax.random.key(seed), 6)
    part_splits = jax.random.split(jax.random.fold_in(streams_of[5], part), 6)
    left_stem = scatter_about(part_splits[0], (2, LROWS, COLS), 1.0, 6.0, ((1, 16),))
    right_stem = scatter_about(part_splits[1], (2, RROWS, COLS), 1.0, 6.0, ((1, 16),))
    branches = scatter_about(streams_of[2], (NBR, 2, 2, BR, BR), (2 * BR) ** -0.5, 0.1875, ((3, 16),))
    slice_bits = place_ends(jax.random.randint(part_splits[3], (NBR,), 0, 2), jax.random.fold_in(part_splits[3], 1), 0, 1).astype(jnp.int32)
    perms = jax.vmap(lambda own: jax.random.permutation(own, NBLK))(jax.random.split(part_splits[4], (LSWEEPS + RSWEEPS))).reshape((LSWEEPS + RSWEEPS, NBLK)).astype(jnp.int32)
    return dict(left_stem=left_stem, right_stem=right_stem, branches=branches, slice_bits=slice_bits, perms=perms)


def column_mix(stem_in, matrix, strided):
    planes, rows, cols = stem_in.shape
    if strided:
        x_real = stem_in[0].astype(jnp.float32).reshape(rows, BR, cols // BR)
        x_imag = stem_in[1].astype(jnp.float32).reshape(rows, BR, cols // BR)
        p_real = matrix[0].astype(jnp.float32)
        p_imag = matrix[1].astype(jnp.float32)
        real_part = jnp.einsum('mcg,cd->mdg', x_real, p_real) - jnp.einsum('mcg,cd->mdg', x_imag, p_imag)
        imag_part = jnp.einsum('mcg,cd->mdg', x_real, p_imag) + jnp.einsum('mcg,cd->mdg', x_imag, p_real)
    else:
        x_real = stem_in[0].reshape(-1, BR)
        x_imag = stem_in[1].reshape(-1, BR)
        real_part = jnp.dot(x_real, matrix[0], preferred_element_type=jnp.float32) - jnp.dot(x_imag, matrix[1], preferred_element_type=jnp.float32)
        imag_part = jnp.dot(x_real, matrix[1], preferred_element_type=jnp.float32) + jnp.dot(x_imag, matrix[0], preferred_element_type=jnp.float32)
    return jnp.stack([real_part, imag_part]).reshape(planes, rows, cols).astype(jnp.bfloat16)

def row_mix(stem_in, matrix, strided):
    planes, rows, cols = stem_in.shape
    groups = rows // BR
    q_real = matrix[0].astype(jnp.float32)
    q_imag = matrix[1].astype(jnp.float32)
    if strided:
        y_real = stem_in[0].astype(jnp.float32).reshape(BR, groups, cols)
        y_imag = stem_in[1].astype(jnp.float32).reshape(BR, groups, cols)
        form = 'rs,sgn->rgn'
    else:
        y_real = stem_in[0].astype(jnp.float32).reshape(groups, BR, cols)
        y_imag = stem_in[1].astype(jnp.float32).reshape(groups, BR, cols)
        form = 'rs,hsn->hrn'
    real_part = jnp.einsum(form, q_real, y_real) - jnp.einsum(form, q_imag, y_imag)
    imag_part = jnp.einsum(form, q_real, y_imag) + jnp.einsum(form, q_imag, y_real)
    return jnp.stack([real_part, imag_part]).reshape(planes, rows, cols).astype(jnp.bfloat16)

def permute(stem_in, block_order):
    planes, rows, cols = stem_in.shape
    blocked = stem_in.reshape(planes, rows, NBLK, BR)
    return jnp.take(blocked, block_order, axis=2).reshape(planes, rows, cols)

def reference(left_stem, right_stem, branches, slice_bits, perms):
    chosen = branches[jnp.arange(NBR, dtype=jnp.int32), slice_bits]
    left = left_stem
    for sweep in range(LSWEEPS):
        strided = sweep % 2 == 1
        left = permute(row_mix(column_mix(left, chosen[2 * sweep], strided), chosen[2 * sweep + 1], strided), perms[sweep])
    right = right_stem
    for sweep in range(LSWEEPS, LSWEEPS + RSWEEPS):
        strided = sweep % 2 == 1
        right = permute(row_mix(column_mix(right, chosen[2 * sweep], strided), chosen[2 * sweep + 1], strided), perms[sweep])
    scale = 1.0 / math.sqrt(2.0 * COLS)
    real_part = jnp.dot(left[0], right[0].T, preferred_element_type=jnp.float32) - jnp.dot(left[1], right[1].T, preferred_element_type=jnp.float32)
    imag_part = jnp.dot(left[0], right[1].T, preferred_element_type=jnp.float32) + jnp.dot(left[1], right[0].T, preferred_element_type=jnp.float32)
    return jnp.stack([real_part, imag_part]) * scale
```

```python
import jax
import jax.numpy as jnp
from jax import lax
from jax.sharding import PartitionSpec as P


def packed(matrix, transposed):
    real, imag = matrix[0], matrix[1]
    if transposed:
        real, imag = real.T, imag.T
    top = jnp.concatenate([real, imag], axis=1)
    bottom = jnp.concatenate([-imag, real], axis=1)
    return jnp.concatenate([top, bottom], axis=0)


def mix(rows_in, matrix, strided, transposed):
    planes, rows, cols = rows_in.shape
    width = matrix.shape[-1]
    groups = cols // width
    if strided:
        grouped = rows_in.reshape(planes, rows, width, groups)
        flat = grouped.transpose(1, 3, 0, 2).reshape(rows * groups, planes * width)
    else:
        grouped = rows_in.reshape(planes, rows, groups, width)
        flat = grouped.transpose(1, 2, 0, 3).reshape(rows * groups, planes * width)
    mixed = jnp.dot(flat, packed(matrix, transposed), preferred_element_type=jnp.float32)
    mixed = mixed.astype(jnp.bfloat16).reshape(rows, groups, planes, width)
    if strided:
        return mixed.transpose(2, 0, 3, 1).reshape(planes, rows, cols)
    return mixed.transpose(2, 0, 1, 3).reshape(planes, rows, cols)


def permute(stem_in, block_order):
    planes, rows, cols = stem_in.shape
    blocks = block_order.shape[0]
    blocked = stem_in.reshape(planes, rows, blocks, cols // blocks)
    return jnp.take(blocked, block_order, axis=2).reshape(planes, rows, cols)


def contract(left, right, dims):
    def dot(a, b):
        return lax.dot_general(a, b, (dims, ((), ())), preferred_element_type=jnp.float32)

    real_part = dot(left[0], right[0]) - dot(left[1], right[1])
    imag_part = dot(left[0], right[1]) + dot(left[1], right[0])
    return jnp.stack([real_part, imag_part])


def shards(left_stem, right_stem, branches, slice_bits, perms):
    left_sweeps = 3
    sweeps = perms.shape[0]

    def own(index):
        return lax.dynamic_index_in_dim(branches[index], slice_bits[index], 0, keepdims=False)

    def fetch(indices):
        stacked = jnp.stack([own(index) for index in indices])
        return lax.all_gather(stacked, "row", axis=2, tiled=True)

    col_mats = fetch([2 * s for s in range(sweeps)])
    row_mats = fetch([2 * s + 1 for s in range(sweeps)])

    stem = right_stem
    for s in range(left_sweeps, sweeps):
        stem = permute(mix(stem, col_mats[s], s % 2 == 1, False), perms[s])
    for s in reversed(range(left_sweeps)):
        stem = permute(stem, jnp.argsort(perms[s]))
        stem = mix(stem, col_mats[s], s % 2 == 1, True)
    gathered = lax.all_gather(stem, "row", axis=1, tiled=True)

    joined = contract(gathered, left_stem, ((1,), (1,))).astype(jnp.bfloat16)
    spread = lax.all_to_all(joined, "row", split_axis=1, concat_axis=2, tiled=True)
    for s in range(left_sweeps):
        spread = mix(spread, row_mats[s], s % 2 == 1, True)
    turned = lax.all_to_all(spread, "row", split_axis=2, concat_axis=1, tiled=True)

    right_rows = row_mats[left_sweeps]
    for s in range(left_sweeps + 1, sweeps):
        right_rows = contract(row_mats[s], right_rows, ((1,), (0,))).astype(jnp.bfloat16)
    scale = (2.0 * left_stem.shape[2]) ** (-0.5)
    return contract(turned, right_rows, ((0,), (1,))) * scale


def solution(mesh):
    in_specs = (
        P(None, ("cuts", "row"), None),
        P(None, ("cuts", "row"), None),
        P(None, None, None, "row", None),
        P("cuts"),
        P("cuts", None),
    )
    out_specs = P(None, ("cuts", "row"), None)
    return jax.shard_map(shards, mesh=mesh, in_specs=in_specs, out_specs=out_specs, check_vma=False)
```

```python
import functools

import jax
import jax.numpy as jnp
from jax import lax
from jax.experimental import pallas as pl
from jax.experimental.pallas import tpu as pltpu
from jax.sharding import PartitionSpec as P


def packed(matrix, transposed):
    real, imag = matrix[0], matrix[1]
    if transposed:
        real, imag = real.T, imag.T
    top = jnp.concatenate([real, imag], axis=1)
    bottom = jnp.concatenate([-imag, real], axis=1)
    return jnp.concatenate([top, bottom], axis=0)


def mix(rows_in, matrix, strided, transposed):
    planes, rows, cols = rows_in.shape
    width = matrix.shape[-1]
    groups = cols // width
    if strided:
        grouped = rows_in.reshape(planes, rows, width, groups)
        flat = grouped.transpose(1, 3, 0, 2).reshape(rows * groups, planes * width)
    else:
        grouped = rows_in.reshape(planes, rows, groups, width)
        flat = grouped.transpose(1, 2, 0, 3).reshape(rows * groups, planes * width)
    mixed = jnp.dot(flat, packed(matrix, transposed), preferred_element_type=jnp.float32)
    mixed = mixed.astype(jnp.bfloat16).reshape(rows, groups, planes, width)
    if strided:
        return mixed.transpose(2, 0, 3, 1).reshape(planes, rows, cols)
    return mixed.transpose(2, 0, 1, 3).reshape(planes, rows, cols)


def permute(stem_in, block_order):
    planes, rows, cols = stem_in.shape
    blocks = block_order.shape[0]
    blocked = stem_in.reshape(planes, rows, blocks, cols // blocks)
    return jnp.take(blocked, block_order, axis=2).reshape(planes, rows, cols)


def contract(left, right, dims):
    def dot(a, b):
        return lax.dot_general(a, b, (dims, ((), ())), preferred_element_type=jnp.float32)

    real_part = dot(left[0], right[0]) - dot(left[1], right[1])
    imag_part = dot(left[0], right[1]) + dot(left[1], right[0])
    return jnp.stack([real_part, imag_part])


def ring_place(index, reach):
    chip = index // 2
    column, level = chip % 2, chip // 2
    return level + column * (2 * reach - 1 - 2 * level)


def ring_device(place, core, reach):
    place = lax.rem(place + 4 * reach, 2 * reach)
    column = place // reach
    level = place + column * (2 * reach - 1 - 2 * place)
    return (level * 2 + column) * 2 + core


class Gather:
    def __init__(self, buf, send_sems, recv_sems, reach):
        self.buf, self.send_sems, self.recv_sems, self.reach = buf, send_sems, recv_sems, reach
        self.me = lax.axis_index("row")
        self.core = self.me % 2
        self.place = ring_place(self.me, reach)
        self.right = ring_device(self.place + 1, self.core, reach)
        self.left = ring_device(self.place - 1, self.core, reach)
        self.twin = self.me + 1 - 2 * self.core

    def origin(self, side, distance, core):
        step = -distance if side == 0 else distance
        return ring_device(self.place + step, core, self.reach)

    def copy(self, origin, half, slot, target):
        ref = self.buf.at[origin] if half is None else self.buf.at[origin, half]
        return pltpu.make_async_remote_copy(
            src_ref=ref, dst_ref=ref,
            send_sem=self.send_sems.at[slot], recv_sem=self.recv_sems.at[slot],
            device_id={"row": target}, device_id_type=pl.DeviceIdType.MESH,
        )

    def ring_copy(self, side, distance):
        half = side if distance == self.reach else None
        origin = self.origin(side, distance - 1, self.core)
        target = self.right if side == 0 else self.left
        return self.copy(origin, half, side * self.reach + distance - 1, target)

    def ring_arrival(self, side, distance):
        half = side if distance == self.reach else None
        origin = self.origin(side, distance, self.core)
        target = self.right if side == 0 else self.left
        return self.copy(origin, half, side * self.reach + distance - 1, target)

    def twin_copy(self, side, distance, core):
        half = side if distance == self.reach else None
        origin = self.origin(side, distance, core)
        slot = 2 * self.reach if distance == 0 else 2 * self.reach + side * self.reach + distance
        return self.copy(origin, half, slot, self.twin)

    def start(self):
        self.ring_copy(0, 1).start()
        self.ring_copy(1, 1).start()
        self.twin_copy(0, 0, self.core).start()

    def step(self, distance):
        for side in (0, 1):
            self.ring_arrival(side, distance).wait_recv()
            if distance < self.reach:
                self.ring_copy(side, distance + 1).start()
            self.twin_copy(side, distance, self.core).start()

    def wait_twin(self, distance):
        for side in (0, 1) if distance else (0,):
            self.twin_copy(side, distance, 1 - self.core).wait_recv()

    def finish(self):
        for distance in range(1, self.reach + 1):
            for side in (0, 1):
                self.ring_copy(side, distance).wait_send()
                self.twin_copy(side, distance, self.core).wait_send()
        self.twin_copy(0, 0, self.core).wait_send()


def cross(a_real, a_imag, w_real, w_imag, transposed):
    dims = (((1,), (1 if transposed else 0,)), ((), ()))

    def dot(a, w):
        return lax.dot_general(a, w, dims, preferred_element_type=jnp.float32)

    return dot(a_real, w_real) - dot(a_imag, w_imag), dot(a_real, w_imag) + dot(a_imag, w_real)


def core_kernel(n, x_hbm, right_ref, branch_ref, bits_ref, order_ref, tt_ref, q_ref,
                pbuf, qbuf, dbuf, xbuf, fbuf, sbuf, acc, x_sem, send_sems, recv_sems):
    reach = n // 4
    me = lax.axis_index("row")
    sweeps = pbuf.shape[2]
    groups, rows, width = fbuf.shape[1:]
    bundle = width // groups
    x_copy = pltpu.make_async_copy(x_hbm, xbuf, x_sem)
    x_copy.start()
    gathers = [
        Gather(buf, send_sems.at[i], recv_sems.at[i], reach)
        for i, buf in enumerate((pbuf, qbuf, dbuf))
    ]
    gp, gq, gd = gathers

    barrier = pltpu.get_barrier_semaphore()
    for other in (gp.right, gp.left, gp.twin):
        pl.semaphore_signal(barrier, inc=1, device_id={"row": other}, device_id_type=pl.DeviceIdType.MESH)
    for s in range(sweeps):
        for plane in (0, 1):
            pbuf[me, plane, s] = branch_ref[2 * s, bits_ref[2 * s], plane]
            qbuf[me, plane, s] = branch_ref[2 * s + 1, bits_ref[2 * s + 1], plane]
    pl.semaphore_wait(barrier, 3)
    gp.start()

    at = lax.broadcasted_iota(jnp.int32, (width, width), 0)
    to = lax.broadcasted_iota(jnp.int32, (width, width), 1)
    turn = (at == (to % bundle) * groups + to // bundle).astype(jnp.bfloat16)

    def turned_rows(w):
        out = lax.dot_general(turn, w, (((0,), (0,)), ((), ())), preferred_element_type=jnp.float32)
        return out.astype(jnp.bfloat16)

    def turned_cols(w):
        return jnp.dot(w, turn, preferred_element_type=jnp.float32).astype(jnp.bfloat16)

    def exchange(index):
        low = lax.broadcasted_iota(jnp.int32, (rows, 2 * bundle), 1) < bundle
        for plane in (0, 1):
            for u in range(groups // 2):
                first = fbuf[plane, index(2 * u)]
                second = fbuf[plane, index(2 * u + 1)]
                there = pl.ds(2 * bundle * u, 2 * bundle)
                for t in range(groups // 2):
                    here = slice(2 * bundle * t, 2 * bundle * (t + 1))
                    a, b = first[:, here], second[:, here]
                    even = jnp.where(low, a, pltpu.roll(b, bundle, 1))
                    odd = jnp.where(low, pltpu.roll(a, bundle, 1), b)
                    sbuf[plane, 2 * t, :, there] = even.astype(jnp.bfloat16)
                    sbuf[plane, 2 * t + 1, :, there] = odd.astype(jnp.bfloat16)

    def operand(index):
        return [
            jnp.concatenate([sbuf[plane, index(g)] for g in range(groups)], axis=0) for plane in (0, 1)
        ]

    def branch(s):
        return [pbuf[:, plane, s].reshape(width, width) for plane in (0, 1)]

    def keep(pair, ref):
        for plane in (0, 1):
            ref[plane] = pair[plane].reshape(groups, rows, width).astype(ref.dtype)

    for plane in (0, 1):
        for g in range(groups):
            block = right_ref[plane, :, pl.ds(g * width, width)]
            fbuf[plane, g] = jnp.dot(block, turn, preferred_element_type=jnp.float32)
    exchange(lambda i: i)

    for d in range(1, reach):
        gp.step(d)
    gq.start()
    gp.step(reach)
    for d in range(reach + 1):
        gp.wait_twin(d)

    keep(cross(*operand(lambda g: g), *branch(3), False), fbuf)
    exchange(lambda i: i)
    w4 = [turned_rows(w) for w in branch(4)]
    keep(cross(*operand(lambda g: order_ref[3, g]), *w4, False), sbuf)
    gq.step(1)
    w2 = [turned_rows(w) for w in branch(2)]
    keep(cross(*operand(lambda g: order_ref[4, order_ref[2, g]]), *w2, True), fbuf)
    exchange(lambda i: order_ref[1, i])
    gq.step(2)
    keep(cross(*operand(lambda g: g), *branch(1), True), fbuf)
    exchange(lambda i: i)
    w0 = [turned_cols(w) for w in branch(0)]
    last = cross(*operand(lambda g: order_ref[0, g]), *w0, True)
    for plane in (0, 1):
        for g in range(groups):
            part = last[plane][g * rows : (g + 1) * rows]
            dbuf[me, plane, :, pl.ds(g * width, width)] = part.astype(jnp.bfloat16)
    gq.step(3)
    gd.start()
    gq.step(reach)
    x_copy.wait()

    def join(origins):
        high = len(origins) * rows
        acc[...] = jnp.zeros_like(acc)

        @pl.loop(0, groups)
        def _(g):
            cols = pl.ds(pl.multiple_of(g * width, width), width)
            a = jnp.concatenate(
                [dbuf[o, plane, :, cols] for plane in (0, 1) for o in origins], axis=0
            )
            dims = (((1,), (1,)), ((), ()))
            for plane in (0, 1):
                acc[plane, : 2 * high] += lax.dot_general(
                    a, xbuf[plane, :, cols], dims, preferred_element_type=jnp.float32
                )

        for i, o in enumerate(origins):
            real = slice(i * rows, (i + 1) * rows)
            imag = slice(high + i * rows, high + (i + 1) * rows)
            tt_ref[o, 0] = (acc[0, real] - acc[1, imag]).astype(tt_ref.dtype)
            tt_ref[o, 1] = (acc[1, real] + acc[0, imag]).astype(tt_ref.dtype)

    gd.wait_twin(0)
    join([me, gd.twin])
    for d in range(1, reach):
        gd.step(d)
        gd.wait_twin(d)
        join([gd.origin(side, d, core) for side in (0, 1) for core in (0, 1)])
    for d in range(reach + 1):
        gq.wait_twin(d)
    q_ref[...] = qbuf[...]
    gd.step(reach)
    gd.wait_twin(reach)
    join([gd.origin(0, reach, core) for core in (0, 1)])
    for gather in gathers:
        gather.finish()


def fused(n, left_stem, right_stem, branches, bits, order):
    planes, tall, cols = left_stem.shape
    rows = right_stem.shape[1]
    part, width = branches.shape[3:]
    sweeps, groups = order.shape
    vmem = pl.BlockSpec(memory_space=pltpu.VMEM)
    smem = pl.BlockSpec(memory_space=pltpu.SMEM)
    bf16 = jnp.bfloat16
    slots = 4 * (n // 4) + 1
    return pl.pallas_call(
        functools.partial(core_kernel, n),
        out_shape=(
            jax.ShapeDtypeStruct((n, planes, rows, tall), bf16),
            jax.ShapeDtypeStruct((n, planes, sweeps, part, width), bf16),
        ),
        in_specs=[pl.BlockSpec(memory_space=pl.ANY), vmem, vmem, smem, smem],
        out_specs=(vmem, vmem),
        scratch_shapes=[
            pltpu.VMEM((n, planes, sweeps, part, width), bf16),
            pltpu.VMEM((n, planes, sweeps, part, width), bf16),
            pltpu.VMEM((n, planes, rows, cols), bf16),
            pltpu.VMEM((planes, tall, cols), bf16),
            pltpu.VMEM((planes, groups, rows, width), jnp.float32),
            pltpu.VMEM((planes, groups, rows, width), bf16),
            pltpu.VMEM((planes, 8 * rows, tall), jnp.float32),
            pltpu.SemaphoreType.DMA,
            pltpu.SemaphoreType.DMA((3, slots)),
            pltpu.SemaphoreType.DMA((3, slots)),
        ],
        compiler_params=pltpu.CompilerParams(
            collective_id=0, has_side_effects=True, vmem_limit_bytes=58 * 2**20
        ),
    )(left_stem, right_stem, branches, bits, order)


def fits(n, right_stem, branches, order):
    part, width = branches.shape[3:]
    groups = order.shape[1]
    return (
        n % 8 == 0 and n // 4 == 4 and part % 16 == 0 and right_stem.shape[1] % 16 == 0
        and width // groups == 64 and n * right_stem.shape[1] == width and order.shape[0] == 5
    )


def shards(n, left_stem, right_stem, branches, slice_bits, perms):
    left_sweeps = 3
    sweeps = perms.shape[0]

    def own(index):
        return lax.dynamic_index_in_dim(branches[index], slice_bits[index], 0, keepdims=False)

    def fetch(indices):
        stacked = jnp.stack([own(index) for index in indices])
        return lax.all_gather(stacked, "row", axis=2, tiled=True)

    if fits(n, right_stem, branches, perms):
        numbers = jnp.arange(perms.shape[1], dtype=jnp.int32)
        hit = (perms[:, None, :] == numbers[None, :, None]).astype(jnp.int32)
        undo = jnp.sum(hit * numbers, axis=2)
        order = jnp.concatenate([undo[:left_sweeps], perms[left_sweeps:]])
        blocks, parts = fused(n, left_stem, right_stem, branches, slice_bits, order)
        joined = blocks.transpose(1, 0, 2, 3).reshape(2, -1, left_stem.shape[1])
        width = branches.shape[-1]
        row_mats = parts.transpose(2, 1, 0, 3, 4).reshape(sweeps, 2, width, width)
    else:
        row_mats = fetch([2 * s + 1 for s in range(sweeps)])
        col_mats = fetch([2 * s for s in range(sweeps)])
        stem = right_stem
        for s in range(left_sweeps, sweeps):
            stem = permute(mix(stem, col_mats[s], s % 2 == 1, False), perms[s])
        for s in reversed(range(left_sweeps)):
            stem = permute(stem, jnp.argsort(perms[s]))
            stem = mix(stem, col_mats[s], s % 2 == 1, True)
        gathered = lax.all_gather(stem, "row", axis=1, tiled=True)
        joined = contract(gathered, left_stem, ((1,), (1,))).astype(jnp.bfloat16)

    spread = lax.all_to_all(joined, "row", split_axis=1, concat_axis=2, tiled=True)
    for s in range(left_sweeps):
        spread = mix(spread, row_mats[s], s % 2 == 1, True)
    turned = lax.all_to_all(spread, "row", split_axis=2, concat_axis=1, tiled=True)

    right_rows = row_mats[left_sweeps]
    for s in range(left_sweeps + 1, sweeps):
        right_rows = contract(row_mats[s], right_rows, ((1,), (0,))).astype(jnp.bfloat16)
    scale = (2.0 * left_stem.shape[2]) ** (-0.5)
    return contract(turned, right_rows, ((0,), (1,))) * scale


def solution(mesh):
    in_specs = (
        P(None, ("cuts", "row"), None),
        P(None, ("cuts", "row"), None),
        P(None, None, None, "row", None),
        P("cuts"),
        P("cuts", None),
    )
    out_specs = P(None, ("cuts", "row"), None)
    return jax.shard_map(functools.partial(shards, mesh.shape["row"]), mesh=mesh, in_specs=in_specs, out_specs=out_specs, check_vma=False)
```

```python
import functools

import jax
import jax.numpy as jnp
from jax import lax
from jax.experimental import pallas as pl
from jax.experimental.pallas import tpu as pltpu
from jax.sharding import PartitionSpec as P


def packed(matrix, transposed):
    real, imag = matrix[0], matrix[1]
    if transposed:
        real, imag = real.T, imag.T
    top = jnp.concatenate([real, imag], axis=1)
    bottom = jnp.concatenate([-imag, real], axis=1)
    return jnp.concatenate([top, bottom], axis=0)


def mix(rows_in, matrix, strided, transposed):
    planes, rows, cols = rows_in.shape
    width = matrix.shape[-1]
    groups = cols // width
    if strided:
        grouped = rows_in.reshape(planes, rows, width, groups)
        flat = grouped.transpose(1, 3, 0, 2).reshape(rows * groups, planes * width)
    else:
        grouped = rows_in.reshape(planes, rows, groups, width)
        flat = grouped.transpose(1, 2, 0, 3).reshape(rows * groups, planes * width)
    mixed = jnp.dot(flat, packed(matrix, transposed), preferred_element_type=jnp.float32)
    mixed = mixed.astype(jnp.bfloat16).reshape(rows, groups, planes, width)
    if strided:
        return mixed.transpose(2, 0, 3, 1).reshape(planes, rows, cols)
    return mixed.transpose(2, 0, 1, 3).reshape(planes, rows, cols)


def permute(stem_in, block_order):
    planes, rows, cols = stem_in.shape
    blocks = block_order.shape[0]
    blocked = stem_in.reshape(planes, rows, blocks, cols // blocks)
    return jnp.take(blocked, block_order, axis=2).reshape(planes, rows, cols)


def contract(left, right, dims):
    def dot(a, b):
        return lax.dot_general(a, b, (dims, ((), ())), preferred_element_type=jnp.float32)

    real_part = dot(left[0], right[0]) - dot(left[1], right[1])
    imag_part = dot(left[0], right[1]) + dot(left[1], right[0])
    return jnp.stack([real_part, imag_part])


def ring_place(index, reach):
    chip = index // 2
    column, level = chip % 2, chip // 2
    return level + column * (2 * reach - 1 - 2 * level)


def ring_device(place, core, reach):
    place = lax.rem(place + 4 * reach, 2 * reach)
    column = place // reach
    level = place + column * (2 * reach - 1 - 2 * place)
    return (level * 2 + column) * 2 + core


class Gather:
    def __init__(self, buf, send_sems, recv_sems, reach):
        self.buf, self.send_sems, self.recv_sems, self.reach = buf, send_sems, recv_sems, reach
        self.me = lax.axis_index("row")
        self.core = self.me % 2
        self.place = ring_place(self.me, reach)
        self.right = ring_device(self.place + 1, self.core, reach)
        self.left = ring_device(self.place - 1, self.core, reach)
        self.twin = self.me + 1 - 2 * self.core

    def origin(self, side, distance, core):
        step = -distance if side == 0 else distance
        return ring_device(self.place + step, core, self.reach)

    def copy(self, origin, half, slot, target):
        ref = self.buf.at[origin] if half is None else self.buf.at[origin, half]
        return pltpu.make_async_remote_copy(
            src_ref=ref, dst_ref=ref,
            send_sem=self.send_sems.at[slot], recv_sem=self.recv_sems.at[slot],
            device_id={"row": target}, device_id_type=pl.DeviceIdType.MESH,
        )

    def ring_copy(self, side, distance):
        half = side if distance == self.reach else None
        origin = self.origin(side, distance - 1, self.core)
        target = self.right if side == 0 else self.left
        return self.copy(origin, half, side * self.reach + distance - 1, target)

    def ring_arrival(self, side, distance):
        half = side if distance == self.reach else None
        origin = self.origin(side, distance, self.core)
        target = self.right if side == 0 else self.left
        return self.copy(origin, half, side * self.reach + distance - 1, target)

    def twin_copy(self, side, distance, core):
        half = side if distance == self.reach else None
        origin = self.origin(side, distance, core)
        slot = 2 * self.reach if distance == 0 else 2 * self.reach + side * self.reach + distance
        return self.copy(origin, half, slot, self.twin)

    def start(self):
        self.ring_copy(0, 1).start()
        self.ring_copy(1, 1).start()
        self.twin_copy(0, 0, self.core).start()

    def step(self, distance):
        for side in (0, 1):
            self.ring_arrival(side, distance).wait_recv()
            if distance < self.reach:
                self.ring_copy(side, distance + 1).start()
            self.twin_copy(side, distance, self.core).start()

    def wait_twin(self, distance):
        for side in (0, 1) if distance else (0,):
            self.twin_copy(side, distance, 1 - self.core).wait_recv()

    def finish(self):
        for distance in range(1, self.reach + 1):
            for side in (0, 1):
                self.ring_copy(side, distance).wait_send()
                self.twin_copy(side, distance, self.core).wait_send()
        self.twin_copy(0, 0, self.core).wait_send()


def cross(a_real, a_imag, w_real, w_imag, transposed):
    dims = (((1,), (1 if transposed else 0,)), ((), ()))

    def dot(a, w):
        return lax.dot_general(a, w, dims, preferred_element_type=jnp.float32)

    return dot(a_real, w_real) - dot(a_imag, w_imag), dot(a_real, w_imag) + dot(a_imag, w_real)


def core_kernel(n, scale, x_hbm, right_ref, branch_ref, bits_ref, order_ref, out_ref,
                pbuf, qbuf, dbuf, xbuf, fbuf, sbuf, acc, near, far, wbuf, x_sem,
                send_sems, recv_sems, near_sems, far_sems):
    reach = n // 4
    me = lax.axis_index("row")
    sweeps = pbuf.shape[2]
    groups, rows, width = fbuf.shape[1:]
    bundle = width // groups
    x_copy = pltpu.make_async_copy(x_hbm, xbuf, x_sem)
    x_copy.start()
    gathers = [
        Gather(buf, send_sems.at[i], recv_sems.at[i], reach)
        for i, buf in enumerate((pbuf, qbuf, dbuf))
    ]
    gp, gq, gd = gathers

    barrier = pltpu.get_barrier_semaphore()

    @pl.loop(1, n)
    def _(i):
        pl.semaphore_signal(
            barrier, inc=1, device_id={"row": lax.rem(me + i, n)}, device_id_type=pl.DeviceIdType.MESH
        )

    for s in range(sweeps):
        for plane in (0, 1):
            pbuf[me, plane, s] = branch_ref[2 * s, bits_ref[2 * s], plane]
            qbuf[me, plane, s] = branch_ref[2 * s + 1, bits_ref[2 * s + 1], plane]
    pl.semaphore_wait(barrier, n - 1)
    gp.start()

    at = lax.broadcasted_iota(jnp.int32, (width, width), 0)
    to = lax.broadcasted_iota(jnp.int32, (width, width), 1)
    turn = (at == (to % bundle) * groups + to // bundle).astype(jnp.bfloat16)

    def turned_rows(w):
        out = lax.dot_general(turn, w, (((0,), (0,)), ((), ())), preferred_element_type=jnp.float32)
        return out.astype(jnp.bfloat16)

    def turned_cols(w):
        return jnp.dot(w, turn, preferred_element_type=jnp.float32).astype(jnp.bfloat16)

    def exchange(index):
        low = lax.broadcasted_iota(jnp.int32, (rows, 2 * bundle), 1) < bundle
        for plane in (0, 1):
            for u in range(groups // 2):
                first = fbuf[plane, index(2 * u)]
                second = fbuf[plane, index(2 * u + 1)]
                there = pl.ds(2 * bundle * u, 2 * bundle)
                for t in range(groups // 2):
                    here = slice(2 * bundle * t, 2 * bundle * (t + 1))
                    a, b = first[:, here], second[:, here]
                    even = jnp.where(low, a, pltpu.roll(b, bundle, 1))
                    odd = jnp.where(low, pltpu.roll(a, bundle, 1), b)
                    sbuf[plane, 2 * t, :, there] = even.astype(jnp.bfloat16)
                    sbuf[plane, 2 * t + 1, :, there] = odd.astype(jnp.bfloat16)

    def operand(index):
        return [
            jnp.concatenate([sbuf[plane, index(g)] for g in range(groups)], axis=0) for plane in (0, 1)
        ]

    def branch(s):
        return [pbuf[:, plane, s].reshape(width, width) for plane in (0, 1)]

    def keep(pair, ref):
        for plane in (0, 1):
            ref[plane] = pair[plane].reshape(groups, rows, width).astype(ref.dtype)

    for plane in (0, 1):
        for g in range(groups):
            block = right_ref[plane, :, pl.ds(g * width, width)]
            fbuf[plane, g] = jnp.dot(block, turn, preferred_element_type=jnp.float32)
    exchange(lambda i: i)

    for d in range(1, reach):
        gp.step(d)
    gq.start()
    gp.step(reach)
    for d in range(reach + 1):
        gp.wait_twin(d)

    keep(cross(*operand(lambda g: g), *branch(3), False), fbuf)
    exchange(lambda i: i)
    w4 = [turned_rows(w) for w in branch(4)]
    keep(cross(*operand(lambda g: order_ref[3, g]), *w4, False), sbuf)
    gq.step(1)
    w2 = [turned_rows(w) for w in branch(2)]
    keep(cross(*operand(lambda g: order_ref[4, order_ref[2, g]]), *w2, True), fbuf)
    exchange(lambda i: order_ref[1, i])
    gq.step(2)
    keep(cross(*operand(lambda g: g), *branch(1), True), fbuf)
    exchange(lambda i: i)
    w0 = [turned_cols(w) for w in branch(0)]
    last = cross(*operand(lambda g: order_ref[0, g]), *w0, True)
    for plane in (0, 1):
        for g in range(groups):
            part = last[plane][g * rows : (g + 1) * rows]
            dbuf[me, plane, :, pl.ds(g * width, width)] = part.astype(jnp.bfloat16)
    gq.step(3)
    gd.start()
    gq.step(reach)
    x_copy.wait()

    def join(origins, own=False):
        high = len(origins) * rows
        acc[...] = jnp.zeros_like(acc)

        @pl.loop(0, groups)
        def _(g):
            cols = pl.ds(pl.multiple_of(g * width, width), width)
            a = jnp.concatenate(
                [dbuf[o, plane, :, cols] for plane in (0, 1) for o in origins], axis=0
            )
            dims = (((1,), (1,)), ((), ()))
            for plane in (0, 1):
                acc[plane, : 2 * high] += lax.dot_general(
                    a, xbuf[plane, :, cols], dims, preferred_element_type=jnp.float32
                )

        for i, o in enumerate(origins):
            real = slice(i * rows, (i + 1) * rows)
            imag = slice(high + i * rows, high + (i + 1) * rows)
            near[turn_one, o, 0] = (acc[0, real] - acc[1, imag]).astype(near.dtype)
            near[turn_one, o, 1] = (acc[1, real] + acc[0, imag]).astype(near.dtype)
            if not (own and i == 0):
                trade(turn_one, o, o).start()

    turn_one, turn_two = 0, 1

    def trade(turn_at, target, slot):
        return pltpu.make_async_remote_copy(
            src_ref=near.at[turn_at, target], dst_ref=far.at[turn_at, me],
            send_sem=near_sems.at[turn_at, slot], recv_sem=far_sems.at[turn_at, me],
            device_id={"row": target}, device_id_type=pl.DeviceIdType.MESH,
        )

    def arrival(turn_at, source):
        return pltpu.make_async_remote_copy(
            src_ref=near.at[turn_at, source], dst_ref=far.at[turn_at, source],
            send_sem=near_sems.at[turn_at, source], recv_sem=far_sems.at[turn_at, source],
            device_id={"row": source}, device_id_type=pl.DeviceIdType.MESH,
        )

    def arrivals(turn_at):
        far[turn_at, me] = near[turn_at, me]

        @pl.loop(1, n)
        def _(i):
            arrival(turn_at, lax.rem(me + i, n)).wait_recv()

    gd.wait_twin(0)
    join([me, gd.twin], own=True)
    for d in range(1, reach):
        gd.step(d)
        gd.wait_twin(d)
        join([gd.origin(side, d, core) for side in (0, 1) for core in (0, 1)])
    for d in range(reach + 1):
        gq.wait_twin(d)

    def row_factor(s):
        return [qbuf[:, plane, s].reshape(width, width) for plane in (0, 1)]

    q1 = [turned_rows(w) for w in row_factor(0)]
    q5 = [turned_cols(w) for w in row_factor(2)]
    ends = cross(*row_factor(4), *row_factor(3), False)
    for plane in (0, 1):
        wbuf[0, plane] = q1[plane]
        wbuf[1, plane] = q5[plane]
        wbuf[2, plane] = ends[plane].astype(wbuf.dtype)
    gd.step(reach)
    gd.wait_twin(reach)
    join([gd.origin(0, reach, core) for core in (0, 1)])
    arrivals(turn_one)

    pieces = n // groups
    whole = [
        jnp.concatenate(
            [
                jnp.concatenate([far[turn_one, g * pieces + i, plane] for i in range(pieces)], axis=1)
                for g in range(groups)
            ],
            axis=0,
        )
        for plane in (0, 1)
    ]
    keep(cross(*whole, wbuf[0, 0], wbuf[0, 1], True), fbuf)
    exchange(lambda i: i)
    keep(cross(*operand(lambda g: g), *row_factor(1), True), fbuf)
    exchange(lambda i: i)
    mixed = cross(*operand(lambda g: g), wbuf[1, 0], wbuf[1, 1], True)
    tall = width // pieces
    for plane in (0, 1):
        for o in range(n):
            g, i = o // pieces, o % pieces
            block = mixed[plane][g * rows : (g + 1) * rows, i * tall : (i + 1) * tall]
            near[turn_two, o, plane] = block.astype(near.dtype)

    @pl.loop(1, n)
    def _(i):
        target = lax.rem(me + i, n)
        trade(turn_two, target, target).start()

    arrivals(turn_two)

    amplitude = cross(
        *[far[turn_two, :, plane].reshape(width, tall).T for plane in (0, 1)],
        wbuf[2, 0], wbuf[2, 1], True,
    )
    for plane in (0, 1):
        out_ref[plane] = amplitude[plane] * scale

    for turn_at in (turn_one, turn_two):

        @pl.loop(1, n)
        def _(i):
            arrival(turn_at, lax.rem(me + i, n)).wait_send()

    for gather in gathers:
        gather.finish()


def fused(n, scale, left_stem, right_stem, branches, bits, order):
    planes, tall, cols = left_stem.shape
    rows = right_stem.shape[1]
    part, width = branches.shape[3:]
    sweeps, groups = order.shape
    vmem = pl.BlockSpec(memory_space=pltpu.VMEM)
    smem = pl.BlockSpec(memory_space=pltpu.SMEM)
    bf16 = jnp.bfloat16
    slots = 4 * (n // 4) + 1
    return pl.pallas_call(
        functools.partial(core_kernel, n, scale),
        out_shape=jax.ShapeDtypeStruct((planes, tall, width), jnp.float32),
        in_specs=[pl.BlockSpec(memory_space=pl.ANY), vmem, vmem, smem, smem],
        out_specs=vmem,
        scratch_shapes=[
            pltpu.VMEM((n, planes, sweeps, part, width), bf16),
            pltpu.VMEM((n, planes, sweeps, part, width), bf16),
            pltpu.VMEM((n, planes, rows, cols), bf16),
            pltpu.VMEM((planes, tall, cols), bf16),
            pltpu.VMEM((planes, groups, rows, width), jnp.float32),
            pltpu.VMEM((planes, groups, rows, width), bf16),
            pltpu.VMEM((planes, 8 * rows, tall), jnp.float32),
            pltpu.VMEM((2, n, planes, rows, tall), bf16),
            pltpu.VMEM((2, n, planes, rows, tall), bf16),
            pltpu.VMEM((3, planes, width, width), bf16),
            pltpu.SemaphoreType.DMA,
            pltpu.SemaphoreType.DMA((3, slots)),
            pltpu.SemaphoreType.DMA((3, slots)),
            pltpu.SemaphoreType.DMA((2, n)),
            pltpu.SemaphoreType.DMA((2, n)),
        ],
        compiler_params=pltpu.CompilerParams(
            collective_id=0, has_side_effects=True, vmem_limit_bytes=58 * 2**20
        ),
    )(left_stem, right_stem, branches, bits, order)


def fits(n, left_stem, right_stem, branches, order):
    part, width = branches.shape[3:]
    groups = order.shape[1]
    return (
        n % 8 == 0 and n // 4 == 4 and part % 16 == 0 and right_stem.shape[1] % 16 == 0
        and width // groups == 64 and n * left_stem.shape[1] == groups * width
        and n % groups == 0 and n * right_stem.shape[1] == width and order.shape[0] == 5
    )


def shards(n, left_stem, right_stem, branches, slice_bits, perms):
    left_sweeps = 3
    sweeps = perms.shape[0]

    scale = (2.0 * left_stem.shape[2]) ** (-0.5)
    if fits(n, left_stem, right_stem, branches, perms):
        numbers = jnp.arange(perms.shape[1], dtype=jnp.int32)
        hit = (perms[:, None, :] == numbers[None, :, None]).astype(jnp.int32)
        undo = jnp.sum(hit * numbers, axis=2)
        order = jnp.concatenate([undo[:left_sweeps], perms[left_sweeps:]])
        return fused(n, scale, left_stem, right_stem, branches, slice_bits, order)

    def own(index):
        return lax.dynamic_index_in_dim(branches[index], slice_bits[index], 0, keepdims=False)

    def fetch(indices):
        stacked = jnp.stack([own(index) for index in indices])
        return lax.all_gather(stacked, "row", axis=2, tiled=True)

    row_mats = fetch([2 * s + 1 for s in range(sweeps)])
    col_mats = fetch([2 * s for s in range(sweeps)])
    stem = right_stem
    for s in range(left_sweeps, sweeps):
        stem = permute(mix(stem, col_mats[s], s % 2 == 1, False), perms[s])
    for s in reversed(range(left_sweeps)):
        stem = permute(stem, jnp.argsort(perms[s]))
        stem = mix(stem, col_mats[s], s % 2 == 1, True)
    gathered = lax.all_gather(stem, "row", axis=1, tiled=True)
    joined = contract(gathered, left_stem, ((1,), (1,))).astype(jnp.bfloat16)

    spread = lax.all_to_all(joined, "row", split_axis=1, concat_axis=2, tiled=True)
    for s in range(left_sweeps):
        spread = mix(spread, row_mats[s], s % 2 == 1, True)
    turned = lax.all_to_all(spread, "row", split_axis=2, concat_axis=1, tiled=True)

    right_rows = row_mats[left_sweeps]
    for s in range(left_sweeps + 1, sweeps):
        right_rows = contract(row_mats[s], right_rows, ((1,), (0,))).astype(jnp.bfloat16)
    return contract(turned, right_rows, ((0,), (1,))) * scale


def solution(mesh):
    in_specs = (
        P(None, ("cuts", "row"), None),
        P(None, ("cuts", "row"), None),
        P(None, None, None, "row", None),
        P("cuts"),
        P("cuts", None),
    )
    out_specs = P(None, ("cuts", "row"), None)
    return jax.shard_map(functools.partial(shards, mesh.shape["row"]), mesh=mesh, in_specs=in_specs, out_specs=out_specs, check_vma=False)
```

```python
import functools

import jax
import jax.numpy as jnp
from jax import lax
from jax.experimental import pallas as pl
from jax.experimental.pallas import tpu as pltpu
from jax.sharding import PartitionSpec as P


def packed(matrix, transposed):
    real, imag = matrix[0], matrix[1]
    if transposed:
        real, imag = real.T, imag.T
    top = jnp.concatenate([real, imag], axis=1)
    bottom = jnp.concatenate([-imag, real], axis=1)
    return jnp.concatenate([top, bottom], axis=0)


def mix(rows_in, matrix, strided, transposed):
    planes, rows, cols = rows_in.shape
    width = matrix.shape[-1]
    groups = cols // width
    if strided:
        grouped = rows_in.reshape(planes, rows, width, groups)
        flat = grouped.transpose(1, 3, 0, 2).reshape(rows * groups, planes * width)
    else:
        grouped = rows_in.reshape(planes, rows, groups, width)
        flat = grouped.transpose(1, 2, 0, 3).reshape(rows * groups, planes * width)
    mixed = jnp.dot(flat, packed(matrix, transposed), preferred_element_type=jnp.float32)
    mixed = mixed.astype(jnp.bfloat16).reshape(rows, groups, planes, width)
    if strided:
        return mixed.transpose(2, 0, 3, 1).reshape(planes, rows, cols)
    return mixed.transpose(2, 0, 1, 3).reshape(planes, rows, cols)


def permute(stem_in, block_order):
    planes, rows, cols = stem_in.shape
    blocks = block_order.shape[0]
    blocked = stem_in.reshape(planes, rows, blocks, cols // blocks)
    return jnp.take(blocked, block_order, axis=2).reshape(planes, rows, cols)


def contract(left, right, dims):
    def dot(a, b):
        return lax.dot_general(a, b, (dims, ((), ())), preferred_element_type=jnp.float32)

    real_part = dot(left[0], right[0]) - dot(left[1], right[1])
    imag_part = dot(left[0], right[1]) + dot(left[1], right[0])
    return jnp.stack([real_part, imag_part])


def ring_place(index, reach):
    chip = index // 2
    column, level = chip % 2, chip // 2
    return level + column * (2 * reach - 1 - 2 * level)


def ring_device(place, core, reach):
    place = lax.rem(place + 4 * reach, 2 * reach)
    column = place // reach
    level = place + column * (2 * reach - 1 - 2 * place)
    return (level * 2 + column) * 2 + core


class Gather:
    def __init__(self, buf, send_sems, recv_sems, reach):
        self.buf, self.send_sems, self.recv_sems, self.reach = buf, send_sems, recv_sems, reach
        self.me = lax.axis_index("row")
        self.core = self.me % 2
        self.place = ring_place(self.me, reach)
        self.right = ring_device(self.place + 1, self.core, reach)
        self.left = ring_device(self.place - 1, self.core, reach)
        self.twin = self.me + 1 - 2 * self.core

    def origin(self, side, distance, core):
        step = -distance if side == 0 else distance
        return ring_device(self.place + step, core, self.reach)

    def copy(self, origin, plane, slot, target):
        ref = self.buf.at[origin, plane]
        return pltpu.make_async_remote_copy(
            src_ref=ref, dst_ref=ref,
            send_sem=self.send_sems.at[slot], recv_sem=self.recv_sems.at[slot],
            device_id={"row": target}, device_id_type=pl.DeviceIdType.MESH,
        )

    def planes(self, side, distance):
        return (side,) if distance == self.reach else (0, 1)

    def slot(self, side, distance, plane):
        return (side * self.reach + distance - 1) * 2 + plane

    def ring_copy(self, side, distance, plane):
        origin = self.origin(side, distance - 1, self.core)
        target = self.right if side == 0 else self.left
        return self.copy(origin, plane, self.slot(side, distance, plane), target)

    def ring_arrival(self, side, distance, plane):
        origin = self.origin(side, distance, self.core)
        target = self.right if side == 0 else self.left
        return self.copy(origin, plane, self.slot(side, distance, plane), target)

    def twin_copy(self, side, distance, plane, core):
        origin = self.origin(side, distance, core)
        past = 4 * self.reach
        slot = past + plane if distance == 0 else past + 2 + self.slot(side, distance, plane)
        return self.copy(origin, plane, slot, self.twin)

    def start(self):
        for plane in (0, 1):
            self.ring_copy(0, 1, plane).start()
            self.ring_copy(1, 1, plane).start()
        for plane in (0, 1):
            self.twin_copy(0, 0, plane, self.core).start()

    def step(self, distance):
        for plane in (0, 1):
            for side in (0, 1):
                if plane in self.planes(side, distance):
                    self.ring_arrival(side, distance, plane).wait_recv()
                    if distance < self.reach and plane in self.planes(side, distance + 1):
                        self.ring_copy(side, distance + 1, plane).start()
                    self.twin_copy(side, distance, plane, self.core).start()

    def wait_twin(self, distance):
        for side in (0, 1) if distance else (0,):
            for plane in self.planes(side, distance):
                self.twin_copy(side, distance, plane, 1 - self.core).wait_recv()

    def finish(self):
        for distance in range(1, self.reach + 1):
            for side in (0, 1):
                for plane in self.planes(side, distance):
                    self.ring_copy(side, distance, plane).wait_send()
                    self.twin_copy(side, distance, plane, self.core).wait_send()
        for plane in (0, 1):
            self.twin_copy(0, 0, plane, self.core).wait_send()


def cross(a_real, a_imag, w_real, w_imag, transposed):
    dims = (((1,), (1 if transposed else 0,)), ((), ()))

    def dot(a, w):
        return lax.dot_general(a, w, dims, preferred_element_type=jnp.float32)

    return dot(a_real, w_real) - dot(a_imag, w_imag), dot(a_real, w_imag) + dot(a_imag, w_real)


def core_kernel(n, scale, x_hbm, right_ref, branch_ref, bits_ref, order_ref, out_ref,
                pbuf, qbuf, dbuf, xbuf, fbuf, sbuf, acc, near, far, wbuf, x_sem,
                send_sems, recv_sems, near_sems, far_sems):
    reach = n // 4
    me = lax.axis_index("row")
    sweeps = pbuf.shape[2]
    groups, rows, width = fbuf.shape[1:]
    bundle = width // groups
    x_copy = pltpu.make_async_copy(x_hbm, xbuf, x_sem)
    x_copy.start()
    gathers = [
        Gather(buf, send_sems.at[i], recv_sems.at[i], reach)
        for i, buf in enumerate((pbuf, qbuf, dbuf))
    ]
    gp, gq, gd = gathers

    barrier = pltpu.get_barrier_semaphore()

    @pl.loop(1, n)
    def _(i):
        pl.semaphore_signal(
            barrier, inc=1, device_id={"row": lax.rem(me + i, n)}, device_id_type=pl.DeviceIdType.MESH
        )

    for s in range(sweeps):
        for plane in (0, 1):
            pbuf[me, plane, s] = branch_ref[2 * s, bits_ref[2 * s], plane]
            qbuf[me, plane, s] = branch_ref[2 * s + 1, bits_ref[2 * s + 1], plane]
    pl.semaphore_wait(barrier, n - 1)
    gp.start()

    at = lax.broadcasted_iota(jnp.int32, (width, width), 0)
    to = lax.broadcasted_iota(jnp.int32, (width, width), 1)
    turn = (at == (to % bundle) * groups + to // bundle).astype(jnp.bfloat16)

    def turned_rows(w):
        out = lax.dot_general(turn, w, (((0,), (0,)), ((), ())), preferred_element_type=jnp.float32)
        return out.astype(jnp.bfloat16)

    def turned_cols(w):
        return jnp.dot(w, turn, preferred_element_type=jnp.float32).astype(jnp.bfloat16)

    def exchange(index):
        low = lax.broadcasted_iota(jnp.int32, (rows, 2 * bundle), 1) < bundle
        for plane in (0, 1):
            for u in range(groups // 2):
                first = fbuf[plane, index(2 * u)]
                second = fbuf[plane, index(2 * u + 1)]
                there = pl.ds(2 * bundle * u, 2 * bundle)
                for t in range(groups // 2):
                    here = slice(2 * bundle * t, 2 * bundle * (t + 1))
                    a, b = first[:, here], second[:, here]
                    even = jnp.where(low, a, pltpu.roll(b, bundle, 1))
                    odd = jnp.where(low, pltpu.roll(a, bundle, 1), b)
                    sbuf[plane, 2 * t, :, there] = even.astype(jnp.bfloat16)
                    sbuf[plane, 2 * t + 1, :, there] = odd.astype(jnp.bfloat16)

    def operand(index):
        return [
            jnp.concatenate([sbuf[plane, index(g)] for g in range(groups)], axis=0) for plane in (0, 1)
        ]

    def branch(s):
        return [pbuf[:, plane, s].reshape(width, width) for plane in (0, 1)]

    def keep(pair, ref):
        for plane in (0, 1):
            ref[plane] = pair[plane].reshape(groups, rows, width).astype(ref.dtype)

    for plane in (0, 1):
        for g in range(groups):
            block = right_ref[plane, :, pl.ds(g * width, width)]
            fbuf[plane, g] = jnp.dot(block, turn, preferred_element_type=jnp.float32)
    exchange(lambda i: i)

    for d in range(1, reach):
        gp.step(d)
    gq.start()
    gp.step(reach)
    for d in range(reach + 1):
        gp.wait_twin(d)

    keep(cross(*operand(lambda g: g), *branch(3), False), fbuf)
    exchange(lambda i: i)
    w4 = [turned_rows(w) for w in branch(4)]
    keep(cross(*operand(lambda g: order_ref[3, g]), *w4, False), sbuf)
    gq.step(1)
    w2 = [turned_rows(w) for w in branch(2)]
    keep(cross(*operand(lambda g: order_ref[4, order_ref[2, g]]), *w2, True), fbuf)
    exchange(lambda i: order_ref[1, i])
    gq.step(2)
    keep(cross(*operand(lambda g: g), *branch(1), True), fbuf)
    exchange(lambda i: i)
    w0 = [turned_cols(w) for w in branch(0)]
    last = cross(*operand(lambda g: order_ref[0, g]), *w0, True)
    for plane in (0, 1):
        for g in range(groups):
            part = last[plane][g * rows : (g + 1) * rows]
            dbuf[me, plane, :, pl.ds(g * width, width)] = part.astype(jnp.bfloat16)
    gd.start()
    gq.step(3)
    gq.step(reach)
    x_copy.wait()

    def join(origins, own=False):
        high = len(origins) * rows
        acc[...] = jnp.zeros_like(acc)

        @pl.loop(0, groups)
        def _(g):
            cols = pl.ds(pl.multiple_of(g * width, width), width)
            a = jnp.concatenate(
                [dbuf[o, plane, :, cols] for plane in (0, 1) for o in origins], axis=0
            )
            dims = (((1,), (1,)), ((), ()))
            for plane in (0, 1):
                acc[plane, : 2 * high] += lax.dot_general(
                    a, xbuf[plane, :, cols], dims, preferred_element_type=jnp.float32
                )

        for i, o in enumerate(origins):
            real = slice(i * rows, (i + 1) * rows)
            imag = slice(high + i * rows, high + (i + 1) * rows)
            near[turn_one, o, 0] = (acc[0, real] - acc[1, imag]).astype(near.dtype)
            near[turn_one, o, 1] = (acc[1, real] + acc[0, imag]).astype(near.dtype)
            if not (own and i == 0):
                trade(turn_one, o, o).start()

    turn_one, turn_two = 0, 1

    def trade(turn_at, target, slot):
        return pltpu.make_async_remote_copy(
            src_ref=near.at[turn_at, target], dst_ref=far.at[turn_at, me],
            send_sem=near_sems.at[turn_at, slot], recv_sem=far_sems.at[turn_at, me],
            device_id={"row": target}, device_id_type=pl.DeviceIdType.MESH,
        )

    def arrival(turn_at, source):
        return pltpu.make_async_remote_copy(
            src_ref=near.at[turn_at, source], dst_ref=far.at[turn_at, source],
            send_sem=near_sems.at[turn_at, source], recv_sem=far_sems.at[turn_at, source],
            device_id={"row": source}, device_id_type=pl.DeviceIdType.MESH,
        )

    def arrivals(turn_at):
        far[turn_at, me] = near[turn_at, me]

        @pl.loop(1, n)
        def _(i):
            arrival(turn_at, lax.rem(me + i, n)).wait_recv()

    gd.wait_twin(0)
    join([me, gd.twin], own=True)
    for d in range(1, reach):
        gd.step(d)
        gd.wait_twin(d)
        join([gd.origin(side, d, core) for side in (0, 1) for core in (0, 1)])
    for d in range(reach + 1):
        gq.wait_twin(d)

    def row_factor(s):
        return [qbuf[:, plane, s].reshape(width, width) for plane in (0, 1)]

    q1 = [turned_rows(w) for w in row_factor(0)]
    q5 = [turned_cols(w) for w in row_factor(2)]
    ends = cross(*row_factor(4), *row_factor(3), False)
    for plane in (0, 1):
        wbuf[0, plane] = q1[plane]
        wbuf[1, plane] = q5[plane]
        wbuf[2, plane] = ends[plane].astype(wbuf.dtype)
    gd.step(reach)
    gd.wait_twin(reach)
    join([gd.origin(0, reach, core) for core in (0, 1)])
    arrivals(turn_one)

    pieces = n // groups
    whole = [
        jnp.concatenate(
            [
                jnp.concatenate([far[turn_one, g * pieces + i, plane] for i in range(pieces)], axis=1)
                for g in range(groups)
            ],
            axis=0,
        )
        for plane in (0, 1)
    ]
    keep(cross(*whole, wbuf[0, 0], wbuf[0, 1], True), fbuf)
    exchange(lambda i: i)
    keep(cross(*operand(lambda g: g), *row_factor(1), True), fbuf)
    exchange(lambda i: i)
    mixed = cross(*operand(lambda g: g), wbuf[1, 0], wbuf[1, 1], True)
    tall = width // pieces
    for plane in (0, 1):
        for o in range(n):
            g, i = o // pieces, o % pieces
            block = mixed[plane][g * rows : (g + 1) * rows, i * tall : (i + 1) * tall]
            near[turn_two, o, plane] = block.astype(near.dtype)

    @pl.loop(1, n)
    def _(i):
        target = lax.rem(me + i, n)
        trade(turn_two, target, target).start()

    arrivals(turn_two)

    amplitude = cross(
        *[far[turn_two, :, plane].reshape(width, tall).T for plane in (0, 1)],
        wbuf[2, 0], wbuf[2, 1], True,
    )
    for plane in (0, 1):
        out_ref[plane] = amplitude[plane] * scale

    for turn_at in (turn_one, turn_two):

        @pl.loop(1, n)
        def _(i):
            arrival(turn_at, lax.rem(me + i, n)).wait_send()

    for gather in gathers:
        gather.finish()


def fused(n, scale, left_stem, right_stem, branches, bits, order):
    planes, tall, cols = left_stem.shape
    rows = right_stem.shape[1]
    part, width = branches.shape[3:]
    sweeps, groups = order.shape
    vmem = pl.BlockSpec(memory_space=pltpu.VMEM)
    smem = pl.BlockSpec(memory_space=pltpu.SMEM)
    bf16 = jnp.bfloat16
    slots = 8 * (n // 4) + 2
    return pl.pallas_call(
        functools.partial(core_kernel, n, scale),
        out_shape=jax.ShapeDtypeStruct((planes, tall, width), jnp.float32),
        in_specs=[pl.BlockSpec(memory_space=pl.ANY), vmem, vmem, smem, smem],
        out_specs=vmem,
        scratch_shapes=[
            pltpu.VMEM((n, planes, sweeps, part, width), bf16),
            pltpu.VMEM((n, planes, sweeps, part, width), bf16),
            pltpu.VMEM((n, planes, rows, cols), bf16),
            pltpu.VMEM((planes, tall, cols), bf16),
            pltpu.VMEM((planes, groups, rows, width), jnp.float32),
            pltpu.VMEM((planes, groups, rows, width), bf16),
            pltpu.VMEM((planes, 8 * rows, tall), jnp.float32),
            pltpu.VMEM((2, n, planes, rows, tall), bf16),
            pltpu.VMEM((2, n, planes, rows, tall), bf16),
            pltpu.VMEM((3, planes, width, width), bf16),
            pltpu.SemaphoreType.DMA,
            pltpu.SemaphoreType.DMA((3, slots)),
            pltpu.SemaphoreType.DMA((3, slots)),
            pltpu.SemaphoreType.DMA((2, n)),
            pltpu.SemaphoreType.DMA((2, n)),
        ],
        compiler_params=pltpu.CompilerParams(
            collective_id=0, has_side_effects=True, vmem_limit_bytes=58 * 2**20
        ),
    )(left_stem, right_stem, branches, bits, order)


def fits(n, left_stem, right_stem, branches, order):
    part, width = branches.shape[3:]
    groups = order.shape[1]
    return (
        n % 8 == 0 and n // 4 == 4 and part % 16 == 0 and right_stem.shape[1] % 16 == 0
        and width // groups == 64 and n * left_stem.shape[1] == groups * width
        and n % groups == 0 and n * right_stem.shape[1] == width and order.shape[0] == 5
    )


def shards(n, left_stem, right_stem, branches, slice_bits, perms):
    left_sweeps = 3
    sweeps = perms.shape[0]

    scale = (2.0 * left_stem.shape[2]) ** (-0.5)
    if fits(n, left_stem, right_stem, branches, perms):
        numbers = jnp.arange(perms.shape[1], dtype=jnp.int32)
        hit = (perms[:, None, :] == numbers[None, :, None]).astype(jnp.int32)
        undo = jnp.sum(hit * numbers, axis=2)
        order = jnp.concatenate([undo[:left_sweeps], perms[left_sweeps:]])
        return fused(n, scale, left_stem, right_stem, branches, slice_bits, order)

    def own(index):
        return lax.dynamic_index_in_dim(branches[index], slice_bits[index], 0, keepdims=False)

    def fetch(indices):
        stacked = jnp.stack([own(index) for index in indices])
        return lax.all_gather(stacked, "row", axis=2, tiled=True)

    row_mats = fetch([2 * s + 1 for s in range(sweeps)])
    col_mats = fetch([2 * s for s in range(sweeps)])
    stem = right_stem
    for s in range(left_sweeps, sweeps):
        stem = permute(mix(stem, col_mats[s], s % 2 == 1, False), perms[s])
    for s in reversed(range(left_sweeps)):
        stem = permute(stem, jnp.argsort(perms[s]))
        stem = mix(stem, col_mats[s], s % 2 == 1, True)
    gathered = lax.all_gather(stem, "row", axis=1, tiled=True)
    joined = contract(gathered, left_stem, ((1,), (1,))).astype(jnp.bfloat16)

    spread = lax.all_to_all(joined, "row", split_axis=1, concat_axis=2, tiled=True)
    for s in range(left_sweeps):
        spread = mix(spread, row_mats[s], s % 2 == 1, True)
    turned = lax.all_to_all(spread, "row", split_axis=2, concat_axis=1, tiled=True)

    right_rows = row_mats[left_sweeps]
    for s in range(left_sweeps + 1, sweeps):
        right_rows = contract(row_mats[s], right_rows, ((1,), (0,))).astype(jnp.bfloat16)
    return contract(turned, right_rows, ((0,), (1,))) * scale


def solution(mesh):
    in_specs = (
        P(None, ("cuts", "row"), None),
        P(None, ("cuts", "row"), None),
        P(None, None, None, "row", None),
        P("cuts"),
        P("cuts", None),
    )
    out_specs = P(None, ("cuts", "row"), None)
    return jax.shard_map(functools.partial(shards, mesh.shape["row"]), mesh=mesh, in_specs=in_specs, out_specs=out_specs, check_vma=False)
```

```python
import functools

import jax
import jax.numpy as jnp
from jax import lax
from jax.experimental import pallas as pl
from jax.experimental.pallas import tpu as pltpu
from jax.sharding import PartitionSpec as P


def packed(matrix, transposed):
    real, imag = matrix[0], matrix[1]
    if transposed:
        real, imag = real.T, imag.T
    top = jnp.concatenate([real, imag], axis=1)
    bottom = jnp.concatenate([-imag, real], axis=1)
    return jnp.concatenate([top, bottom], axis=0)


def mix(rows_in, matrix, strided, transposed):
    planes, rows, cols = rows_in.shape
    width = matrix.shape[-1]
    groups = cols // width
    if strided:
        grouped = rows_in.reshape(planes, rows, width, groups)
        flat = grouped.transpose(1, 3, 0, 2).reshape(rows * groups, planes * width)
    else:
        grouped = rows_in.reshape(planes, rows, groups, width)
        flat = grouped.transpose(1, 2, 0, 3).reshape(rows * groups, planes * width)
    mixed = jnp.dot(flat, packed(matrix, transposed), preferred_element_type=jnp.float32)
    mixed = mixed.astype(jnp.bfloat16).reshape(rows, groups, planes, width)
    if strided:
        return mixed.transpose(2, 0, 3, 1).reshape(planes, rows, cols)
    return mixed.transpose(2, 0, 1, 3).reshape(planes, rows, cols)


def permute(stem_in, block_order):
    planes, rows, cols = stem_in.shape
    blocks = block_order.shape[0]
    blocked = stem_in.reshape(planes, rows, blocks, cols // blocks)
    return jnp.take(blocked, block_order, axis=2).reshape(planes, rows, cols)


def contract(left, right, dims):
    def dot(a, b):
        return lax.dot_general(a, b, (dims, ((), ())), preferred_element_type=jnp.float32)

    real_part = dot(left[0], right[0]) - dot(left[1], right[1])
    imag_part = dot(left[0], right[1]) + dot(left[1], right[0])
    return jnp.stack([real_part, imag_part])


def ring_place(index, reach):
    chip = index // 2
    column, level = chip % 2, chip // 2
    return level + column * (2 * reach - 1 - 2 * level)


def ring_device(place, core, reach):
    place = lax.rem(place + 4 * reach, 2 * reach)
    column = place // reach
    level = place + column * (2 * reach - 1 - 2 * place)
    return (level * 2 + column) * 2 + core


class Gather:
    def __init__(self, buf, send_sems, recv_sems, reach):
        self.buf, self.send_sems, self.recv_sems, self.reach = buf, send_sems, recv_sems, reach
        self.me = lax.axis_index("row")
        self.core = self.me % 2
        self.place = ring_place(self.me, reach)
        self.right = ring_device(self.place + 1, self.core, reach)
        self.left = ring_device(self.place - 1, self.core, reach)
        self.twin = self.me + 1 - 2 * self.core

    def origin(self, side, distance, core):
        step = -distance if side == 0 else distance
        return ring_device(self.place + step, core, self.reach)

    def copy(self, origin, plane, slot, target):
        ref = self.buf.at[origin, plane]
        return pltpu.make_async_remote_copy(
            src_ref=ref, dst_ref=ref,
            send_sem=self.send_sems.at[slot], recv_sem=self.recv_sems.at[slot],
            device_id={"row": target}, device_id_type=pl.DeviceIdType.MESH,
        )

    def planes(self, side, distance):
        return (side,) if distance == self.reach else (0, 1)

    def slot(self, side, distance, plane):
        return (side * self.reach + distance - 1) * 2 + plane

    def ring_copy(self, side, distance, plane):
        origin = self.origin(side, distance - 1, self.core)
        target = self.right if side == 0 else self.left
        return self.copy(origin, plane, self.slot(side, distance, plane), target)

    def ring_arrival(self, side, distance, plane):
        origin = self.origin(side, distance, self.core)
        target = self.right if side == 0 else self.left
        return self.copy(origin, plane, self.slot(side, distance, plane), target)

    def twin_copy(self, side, distance, plane, core):
        origin = self.origin(side, distance, core)
        past = 4 * self.reach
        slot = past + plane if distance == 0 else past + 2 + self.slot(side, distance, plane)
        return self.copy(origin, plane, slot, self.twin)

    def start(self):
        for plane in (0, 1):
            self.ring_copy(0, 1, plane).start()
            self.ring_copy(1, 1, plane).start()
        for plane in (0, 1):
            self.twin_copy(0, 0, plane, self.core).start()

    def step(self, distance):
        for plane in (0, 1):
            for side in (0, 1):
                if plane in self.planes(side, distance):
                    self.ring_arrival(side, distance, plane).wait_recv()
                    if distance < self.reach and plane in self.planes(side, distance + 1):
                        self.ring_copy(side, distance + 1, plane).start()
                    self.twin_copy(side, distance, plane, self.core).start()

    def wait_twin(self, distance):
        for side in (0, 1) if distance else (0,):
            for plane in self.planes(side, distance):
                self.twin_copy(side, distance, plane, 1 - self.core).wait_recv()

    def finish(self):
        for distance in range(1, self.reach + 1):
            for side in (0, 1):
                for plane in self.planes(side, distance):
                    self.ring_copy(side, distance, plane).wait_send()
                    self.twin_copy(side, distance, plane, self.core).wait_send()
        for plane in (0, 1):
            self.twin_copy(0, 0, plane, self.core).wait_send()


def cross(a_real, a_imag, w_real, w_imag, transposed):
    dims = (((1,), (1 if transposed else 0,)), ((), ()))

    def dot(a, w):
        return lax.dot_general(a, w, dims, preferred_element_type=jnp.float32)

    return dot(a_real, w_real) - dot(a_imag, w_imag), dot(a_real, w_imag) + dot(a_imag, w_real)


def core_kernel(n, x_hbm, right_ref, branch_ref, bits_ref, order_ref, out_ref,
                pbuf, qbuf, dbuf, ebuf, xbuf, fbuf, sbuf, acc, near, far, wbuf, x_sem,
                send_sems, recv_sems, near_sems, far_sems):
    reach = n // 4
    me = lax.axis_index("row")
    sweeps = pbuf.shape[2]
    groups, rows, width = fbuf.shape[1:]
    bundle = width // groups
    x_copy = pltpu.make_async_copy(x_hbm, xbuf, x_sem)
    x_copy.start()
    gathers = [
        Gather(buf, send_sems.at[i], recv_sems.at[i], reach)
        for i, buf in enumerate((pbuf, qbuf, dbuf, ebuf))
    ]
    gp, gq, gd, ge = gathers
    early = qbuf.shape[2]

    barrier = pltpu.get_barrier_semaphore()

    @pl.loop(1, n)
    def _(i):
        pl.semaphore_signal(
            barrier, inc=1, device_id={"row": lax.rem(me + i, n)}, device_id_type=pl.DeviceIdType.MESH
        )

    for s in range(sweeps):
        for plane in (0, 1):
            pbuf[me, plane, s] = branch_ref[2 * s, bits_ref[2 * s], plane]
            row_part = branch_ref[2 * s + 1, bits_ref[2 * s + 1], plane]
            if s < early:
                qbuf[me, plane, s] = row_part
            else:
                ebuf[me, plane, s - early] = row_part
    pl.semaphore_wait(barrier, n - 1)
    gp.start()

    at = lax.broadcasted_iota(jnp.int32, (width, width), 0)
    to = lax.broadcasted_iota(jnp.int32, (width, width), 1)
    turn = (at == (to % bundle) * groups + to // bundle).astype(jnp.bfloat16)

    def turned_rows(w):
        out = lax.dot_general(turn, w, (((0,), (0,)), ((), ())), preferred_element_type=jnp.float32)
        return out.astype(jnp.bfloat16)

    def turned_cols(w):
        return jnp.dot(w, turn, preferred_element_type=jnp.float32).astype(jnp.bfloat16)

    def exchange(index):
        low = lax.broadcasted_iota(jnp.int32, (rows, 2 * bundle), 1) < bundle
        for plane in (0, 1):
            for u in range(groups // 2):
                first = fbuf[plane, index(2 * u)]
                second = fbuf[plane, index(2 * u + 1)]
                there = pl.ds(2 * bundle * u, 2 * bundle)
                for t in range(groups // 2):
                    here = slice(2 * bundle * t, 2 * bundle * (t + 1))
                    a, b = first[:, here], second[:, here]
                    even = jnp.where(low, a, pltpu.roll(b, bundle, 1))
                    odd = jnp.where(low, pltpu.roll(a, bundle, 1), b)
                    sbuf[plane, 2 * t, :, there] = even.astype(jnp.bfloat16)
                    sbuf[plane, 2 * t + 1, :, there] = odd.astype(jnp.bfloat16)

    def operand(index):
        return [
            jnp.concatenate([sbuf[plane, index(g)] for g in range(groups)], axis=0) for plane in (0, 1)
        ]

    def branch(s):
        return [pbuf[:, plane, s].reshape(width, width) for plane in (0, 1)]

    def undo(s, group):
        place = jnp.int32(0)
        for g in range(1, groups):
            place = jnp.where(order_ref[s, g] == group, jnp.int32(g), place)
        return place

    def keep(pair, ref):
        for plane in (0, 1):
            ref[plane] = pair[plane].reshape(groups, rows, width).astype(ref.dtype)

    for plane in (0, 1):
        for g in range(groups):
            block = right_ref[plane, :, pl.ds(g * width, width)]
            fbuf[plane, g] = jnp.dot(block, turn, preferred_element_type=jnp.float32)
    exchange(lambda i: i)

    for d in range(1, reach):
        gp.step(d)
    gq.start()
    gp.step(reach)
    for d in range(reach + 1):
        gp.wait_twin(d)

    keep(cross(*operand(lambda g: g), *branch(3), False), fbuf)
    exchange(lambda i: i)
    w4 = [turned_rows(w) for w in branch(4)]
    keep(cross(*operand(lambda g: order_ref[3, g]), *w4, False), sbuf)
    gq.step(1)
    w2 = [turned_rows(w) for w in branch(2)]
    keep(cross(*operand(lambda g: order_ref[4, undo(2, g)]), *w2, True), fbuf)
    exchange(lambda i: undo(1, i))
    gq.step(2)
    keep(cross(*operand(lambda g: g), *branch(1), True), fbuf)
    exchange(lambda i: i)
    w0 = [turned_cols(w) for w in branch(0)]
    last = cross(*operand(lambda g: undo(0, g)), *w0, True)
    for plane in (0, 1):
        for g in range(groups):
            part = last[plane][g * rows : (g + 1) * rows]
            dbuf[me, plane, :, pl.ds(g * width, width)] = part.astype(jnp.bfloat16)
    gd.start()
    gq.step(3)
    gq.step(reach)
    x_copy.wait()

    def join(origins, own=False):
        high = len(origins) * rows
        acc[...] = jnp.zeros_like(acc)

        @pl.loop(0, groups)
        def _(g):
            cols = pl.ds(pl.multiple_of(g * width, width), width)
            a = jnp.concatenate(
                [dbuf[o, plane, :, cols] for plane in (0, 1) for o in origins], axis=0
            )
            dims = (((1,), (1,)), ((), ()))
            for plane in (0, 1):
                acc[plane, : 2 * high] += lax.dot_general(
                    a, xbuf[plane, :, cols], dims, preferred_element_type=jnp.float32
                )

        for i, o in enumerate(origins):
            real = slice(i * rows, (i + 1) * rows)
            imag = slice(high + i * rows, high + (i + 1) * rows)
            near[turn_one, o, 0] = (acc[0, real] - acc[1, imag]).astype(near.dtype)
            near[turn_one, o, 1] = (acc[1, real] + acc[0, imag]).astype(near.dtype)
            if not (own and i == 0):
                trade(turn_one, o, o).start()

    turn_one, turn_two = 0, 1

    def trade(turn_at, target, slot):
        return pltpu.make_async_remote_copy(
            src_ref=near.at[turn_at, target], dst_ref=far.at[turn_at, me],
            send_sem=near_sems.at[turn_at, slot], recv_sem=far_sems.at[turn_at, me],
            device_id={"row": target}, device_id_type=pl.DeviceIdType.MESH,
        )

    def arrival(turn_at, source):
        return pltpu.make_async_remote_copy(
            src_ref=near.at[turn_at, source], dst_ref=far.at[turn_at, source],
            send_sem=near_sems.at[turn_at, source], recv_sem=far_sems.at[turn_at, source],
            device_id={"row": source}, device_id_type=pl.DeviceIdType.MESH,
        )

    def arrivals(turn_at):
        far[turn_at, me] = near[turn_at, me]

        @pl.loop(1, n)
        def _(i):
            arrival(turn_at, lax.rem(me + i, n)).wait_recv()

    gd.wait_twin(0)
    join([me, gd.twin], own=True)
    for d in range(1, reach):
        gd.step(d)
        if d == reach - 1:
            ge.start()
        gd.wait_twin(d)
        join([gd.origin(side, d, core) for side in (0, 1) for core in (0, 1)])
    for d in range(reach + 1):
        gq.wait_twin(d)

    def row_factor(s):
        buf, at = (qbuf, s) if s < early else (ebuf, s - early)
        return [buf[:, plane, at].reshape(width, width) for plane in (0, 1)]

    q1 = [turned_rows(w) for w in row_factor(0)]
    q5 = [turned_cols(w) for w in row_factor(2)]
    for plane in (0, 1):
        wbuf[0, plane] = q1[plane]
        wbuf[1, plane] = q5[plane]
    gd.step(reach)
    gd.wait_twin(reach)
    join([gd.origin(0, reach, core) for core in (0, 1)])
    ge.step(1)
    arrivals(turn_one)

    pieces = n // groups
    whole = [
        jnp.concatenate(
            [
                jnp.concatenate([far[turn_one, g * pieces + i, plane] for i in range(pieces)], axis=1)
                for g in range(groups)
            ],
            axis=0,
        )
        for plane in (0, 1)
    ]
    keep(cross(*whole, wbuf[0, 0], wbuf[0, 1], True), fbuf)
    exchange(lambda i: i)
    ge.step(2)
    keep(cross(*operand(lambda g: g), *row_factor(1), True), fbuf)
    exchange(lambda i: i)
    ge.step(3)
    mixed = cross(*operand(lambda g: g), wbuf[1, 0], wbuf[1, 1], True)
    tall = width // pieces
    for plane in (0, 1):
        for o in range(n):
            g, i = o // pieces, o % pieces
            block = mixed[plane][g * rows : (g + 1) * rows, i * tall : (i + 1) * tall]
            near[turn_two, o, plane] = block.astype(near.dtype)

    @pl.loop(1, n)
    def _(i):
        target = lax.rem(me + i, n)
        trade(turn_two, target, target).start()

    ge.step(reach)
    for d in range(reach + 1):
        ge.wait_twin(d)
    ends = cross(*row_factor(4), *row_factor(3), False)
    for plane in (0, 1):
        wbuf[2, plane] = ends[plane].astype(wbuf.dtype)
    arrivals(turn_two)

    amplitude = cross(
        *[far[turn_two, :, plane].reshape(width, tall).T for plane in (0, 1)],
        wbuf[2, 0], wbuf[2, 1], True,
    )
    for plane in (0, 1):
        out_ref[plane] = amplitude[plane]

    for turn_at in (turn_one, turn_two):

        @pl.loop(1, n)
        def _(i):
            arrival(turn_at, lax.rem(me + i, n)).wait_send()

    for gather in gathers:
        gather.finish()


def fused(n, left_stem, right_stem, branches, bits, order):
    planes, tall, cols = left_stem.shape
    rows = right_stem.shape[1]
    part, width = branches.shape[3:]
    sweeps, groups = order.shape
    vmem = pl.BlockSpec(memory_space=pltpu.VMEM)
    smem = pl.BlockSpec(memory_space=pltpu.SMEM)
    bf16 = jnp.bfloat16
    slots = 8 * (n // 4) + 2
    return pl.pallas_call(
        functools.partial(core_kernel, n),
        out_shape=jax.ShapeDtypeStruct((planes, tall, width), jnp.float32),
        in_specs=[pl.BlockSpec(memory_space=pl.ANY), vmem, vmem, smem, smem],
        out_specs=vmem,
        scratch_shapes=[
            pltpu.VMEM((n, planes, sweeps, part, width), bf16),
            pltpu.VMEM((n, planes, 3, part, width), bf16),
            pltpu.VMEM((n, planes, rows, cols), bf16),
            pltpu.VMEM((n, planes, sweeps - 3, part, width), bf16),
            pltpu.VMEM((planes, tall, cols), bf16),
            pltpu.VMEM((planes, groups, rows, width), jnp.float32),
            pltpu.VMEM((planes, groups, rows, width), bf16),
            pltpu.VMEM((planes, 8 * rows, tall), jnp.float32),
            pltpu.VMEM((2, n, planes, rows, tall), bf16),
            pltpu.VMEM((2, n, planes, rows, tall), bf16),
            pltpu.VMEM((3, planes, width, width), bf16),
            pltpu.SemaphoreType.DMA,
            pltpu.SemaphoreType.DMA((4, slots)),
            pltpu.SemaphoreType.DMA((4, slots)),
            pltpu.SemaphoreType.DMA((2, n)),
            pltpu.SemaphoreType.DMA((2, n)),
        ],
        compiler_params=pltpu.CompilerParams(
            collective_id=0, has_side_effects=True, vmem_limit_bytes=58 * 2**20
        ),
    )(left_stem, right_stem, branches, bits, order)


def fits(n, left_stem, right_stem, branches, order):
    part, width = branches.shape[3:]
    groups = order.shape[1]
    return (
        n % 8 == 0 and n // 4 == 4 and part % 16 == 0 and right_stem.shape[1] % 16 == 0
        and width // groups == 64 and n * left_stem.shape[1] == groups * width
        and n % groups == 0 and n * right_stem.shape[1] == width and order.shape[0] == 5
    )


def shards(n, left_stem, right_stem, branches, slice_bits, perms):
    left_sweeps = 3
    sweeps = perms.shape[0]

    scale = (2.0 * left_stem.shape[2]) ** (-0.5)
    if fits(n, left_stem, right_stem, branches, perms):
        return fused(n, left_stem, right_stem, branches, slice_bits, perms) * scale

    def own(index):
        return lax.dynamic_index_in_dim(branches[index], slice_bits[index], 0, keepdims=False)

    def fetch(indices):
        stacked = jnp.stack([own(index) for index in indices])
        return lax.all_gather(stacked, "row", axis=2, tiled=True)

    row_mats = fetch([2 * s + 1 for s in range(sweeps)])
    col_mats = fetch([2 * s for s in range(sweeps)])
    stem = right_stem
    for s in range(left_sweeps, sweeps):
        stem = permute(mix(stem, col_mats[s], s % 2 == 1, False), perms[s])
    for s in reversed(range(left_sweeps)):
        stem = permute(stem, jnp.argsort(perms[s]))
        stem = mix(stem, col_mats[s], s % 2 == 1, True)
    gathered = lax.all_gather(stem, "row", axis=1, tiled=True)
    joined = contract(gathered, left_stem, ((1,), (1,))).astype(jnp.bfloat16)

    spread = lax.all_to_all(joined, "row", split_axis=1, concat_axis=2, tiled=True)
    for s in range(left_sweeps):
        spread = mix(spread, row_mats[s], s % 2 == 1, True)
    turned = lax.all_to_all(spread, "row", split_axis=2, concat_axis=1, tiled=True)

    right_rows = row_mats[left_sweeps]
    for s in range(left_sweeps + 1, sweeps):
        right_rows = contract(row_mats[s], right_rows, ((1,), (0,))).astype(jnp.bfloat16)
    return contract(turned, right_rows, ((0,), (1,))) * scale


def solution(mesh):
    in_specs = (
        P(None, ("cuts", "row"), None),
        P(None, ("cuts", "row"), None),
        P(None, None, None, "row", None),
        P("cuts"),
        P("cuts", None),
    )
    out_specs = P(None, ("cuts", "row"), None)
    return jax.shard_map(functools.partial(shards, mesh.shape["row"]), mesh=mesh, in_specs=in_specs, out_specs=out_specs, check_vma=False)
```

```python
import functools

import jax
import jax.numpy as jnp
from jax import lax
from jax.experimental import pallas as pl
from jax.experimental.pallas import tpu as pltpu
from jax.sharding import PartitionSpec as P


def packed(matrix, transposed):
    real, imag = matrix[0], matrix[1]
    if transposed:
        real, imag = real.T, imag.T
    top = jnp.concatenate([real, imag], axis=1)
    bottom = jnp.concatenate([-imag, real], axis=1)
    return jnp.concatenate([top, bottom], axis=0)


def mix(rows_in, matrix, strided, transposed):
    planes, rows, cols = rows_in.shape
    width = matrix.shape[-1]
    groups = cols // width
    if strided:
        grouped = rows_in.reshape(planes, rows, width, groups)
        flat = grouped.transpose(1, 3, 0, 2).reshape(rows * groups, planes * width)
    else:
        grouped = rows_in.reshape(planes, rows, groups, width)
        flat = grouped.transpose(1, 2, 0, 3).reshape(rows * groups, planes * width)
    mixed = jnp.dot(flat, packed(matrix, transposed), preferred_element_type=jnp.float32)
    mixed = mixed.astype(jnp.bfloat16).reshape(rows, groups, planes, width)
    if strided:
        return mixed.transpose(2, 0, 3, 1).reshape(planes, rows, cols)
    return mixed.transpose(2, 0, 1, 3).reshape(planes, rows, cols)


def permute(stem_in, block_order):
    planes, rows, cols = stem_in.shape
    blocks = block_order.shape[0]
    blocked = stem_in.reshape(planes, rows, blocks, cols // blocks)
    return jnp.take(blocked, block_order, axis=2).reshape(planes, rows, cols)


def contract(left, right, dims):
    def dot(a, b):
        return lax.dot_general(a, b, (dims, ((), ())), preferred_element_type=jnp.float32)

    real_part = dot(left[0], right[0]) - dot(left[1], right[1])
    imag_part = dot(left[0], right[1]) + dot(left[1], right[0])
    return jnp.stack([real_part, imag_part])


def ring_place(index, reach):
    chip = index // 2
    column, level = chip % 2, chip // 2
    return level + column * (2 * reach - 1 - 2 * level)


def ring_device(place, core, reach):
    place = lax.rem(place + 4 * reach, 2 * reach)
    column = place // reach
    level = place + column * (2 * reach - 1 - 2 * place)
    return (level * 2 + column) * 2 + core


class Gather:
    def __init__(self, buf, send_sems, recv_sems, reach):
        self.buf, self.send_sems, self.recv_sems, self.reach = buf, send_sems, recv_sems, reach
        self.me = lax.axis_index("row")
        self.core = self.me % 2
        self.place = ring_place(self.me, reach)
        self.right = ring_device(self.place + 1, self.core, reach)
        self.left = ring_device(self.place - 1, self.core, reach)
        self.twin = self.me + 1 - 2 * self.core

    def origin(self, side, distance, core):
        step = -distance if side == 0 else distance
        return ring_device(self.place + step, core, self.reach)

    def copy(self, origin, plane, slot, target):
        ref = self.buf.at[origin, plane]
        return pltpu.make_async_remote_copy(
            src_ref=ref, dst_ref=ref,
            send_sem=self.send_sems.at[slot], recv_sem=self.recv_sems.at[slot],
            device_id={"row": target}, device_id_type=pl.DeviceIdType.MESH,
        )

    def planes(self, side, distance):
        return (side,) if distance == self.reach else (0, 1)

    def slot(self, side, distance, plane):
        return (side * self.reach + distance - 1) * 2 + plane

    def ring_copy(self, side, distance, plane):
        origin = self.origin(side, distance - 1, self.core)
        target = self.right if side == 0 else self.left
        return self.copy(origin, plane, self.slot(side, distance, plane), target)

    def ring_arrival(self, side, distance, plane):
        origin = self.origin(side, distance, self.core)
        target = self.right if side == 0 else self.left
        return self.copy(origin, plane, self.slot(side, distance, plane), target)

    def twin_copy(self, side, distance, plane, core):
        origin = self.origin(side, distance, core)
        past = 4 * self.reach
        slot = past + plane if distance == 0 else past + 2 + self.slot(side, distance, plane)
        return self.copy(origin, plane, slot, self.twin)

    def start(self):
        for plane in (0, 1):
            self.ring_copy(0, 1, plane).start()
            self.ring_copy(1, 1, plane).start()
        for plane in (0, 1):
            self.twin_copy(0, 0, plane, self.core).start()

    def step(self, distance):
        for plane in (0, 1):
            for side in (0, 1):
                if plane in self.planes(side, distance):
                    self.ring_arrival(side, distance, plane).wait_recv()
                    if distance < self.reach and plane in self.planes(side, distance + 1):
                        self.ring_copy(side, distance + 1, plane).start()
                    self.twin_copy(side, distance, plane, self.core).start()

    def wait_twin(self, distance):
        for side in (0, 1) if distance else (0,):
            for plane in self.planes(side, distance):
                self.twin_copy(side, distance, plane, 1 - self.core).wait_recv()

    def finish(self):
        for distance in range(1, self.reach + 1):
            for side in (0, 1):
                for plane in self.planes(side, distance):
                    self.ring_copy(side, distance, plane).wait_send()
                    self.twin_copy(side, distance, plane, self.core).wait_send()
        for plane in (0, 1):
            self.twin_copy(0, 0, plane, self.core).wait_send()


def cross(a_real, a_imag, w_real, w_imag, transposed):
    dims = (((1,), (1 if transposed else 0,)), ((), ()))

    def dot(a, w):
        return lax.dot_general(a, w, dims, preferred_element_type=jnp.float32)

    return dot(a_real, w_real) - dot(a_imag, w_imag), dot(a_real, w_imag) + dot(a_imag, w_real)


def core_kernel(n, x_hbm, right_ref, branch_ref, bits_ref, order_ref, out_ref,
                pbuf, qbuf, dbuf, ebuf, xbuf, fbuf, sbuf, acc, near, far, wbuf, x_sem,
                send_sems, recv_sems, near_sems, far_sems):
    reach = n // 4
    me = lax.axis_index("row")
    sweeps = pbuf.shape[2]
    groups, rows, width = fbuf.shape[1:]
    bundle = width // groups
    x_copy = pltpu.make_async_copy(x_hbm, xbuf, x_sem)
    x_copy.start()
    gathers = [
        Gather(buf, send_sems.at[i], recv_sems.at[i], reach)
        for i, buf in enumerate((pbuf, qbuf, dbuf, ebuf))
    ]
    gp, gq, gd, ge = gathers
    early = qbuf.shape[2]

    barrier = pltpu.get_barrier_semaphore()

    @pl.loop(1, n)
    def _(i):
        pl.semaphore_signal(
            barrier, inc=1, device_id={"row": lax.rem(me + i, n)}, device_id_type=pl.DeviceIdType.MESH
        )

    for s in range(sweeps):
        for plane in (0, 1):
            pbuf[me, plane, s] = branch_ref[2 * s, bits_ref[2 * s], plane]
            row_part = branch_ref[2 * s + 1, bits_ref[2 * s + 1], plane]
            if s < early:
                qbuf[me, plane, s] = row_part
            else:
                ebuf[me, plane, s - early] = row_part
    pl.semaphore_wait(barrier, n - 1)
    gp.start()

    at = lax.broadcasted_iota(jnp.int32, (width, width), 0)
    to = lax.broadcasted_iota(jnp.int32, (width, width), 1)
    turn = (at == (to % bundle) * groups + to // bundle).astype(jnp.bfloat16)

    def turned_rows(w):
        out = lax.dot_general(turn, w, (((0,), (0,)), ((), ())), preferred_element_type=jnp.float32)
        return out.astype(jnp.bfloat16)

    def turned_cols(w):
        return jnp.dot(w, turn, preferred_element_type=jnp.float32).astype(jnp.bfloat16)

    def exchange(index):
        low = lax.broadcasted_iota(jnp.int32, (rows, 2 * bundle), 1) < bundle
        for plane in (0, 1):
            for u in range(groups // 2):
                first = fbuf[plane, index(2 * u)]
                second = fbuf[plane, index(2 * u + 1)]
                there = pl.ds(2 * bundle * u, 2 * bundle)
                for t in range(groups // 2):
                    here = slice(2 * bundle * t, 2 * bundle * (t + 1))
                    a, b = first[:, here], second[:, here]
                    even = jnp.where(low, a, pltpu.roll(b, bundle, 1))
                    odd = jnp.where(low, pltpu.roll(a, bundle, 1), b)
                    sbuf[plane, 2 * t, :, there] = even.astype(jnp.bfloat16)
                    sbuf[plane, 2 * t + 1, :, there] = odd.astype(jnp.bfloat16)

    def operand(index):
        return [
            jnp.concatenate([sbuf[plane, index(g)] for g in range(groups)], axis=0) for plane in (0, 1)
        ]

    def branch(s):
        return [pbuf[:, plane, s].reshape(width, width) for plane in (0, 1)]

    def undo(s, group):
        place = jnp.int32(0)
        for g in range(1, groups):
            place = jnp.where(order_ref[s, g] == group, jnp.int32(g), place)
        return place

    def keep(pair, ref):
        for plane in (0, 1):
            ref[plane] = pair[plane].reshape(groups, rows, width).astype(ref.dtype)

    for plane in (0, 1):
        for g in range(groups):
            block = right_ref[plane, :, pl.ds(g * width, width)]
            fbuf[plane, g] = jnp.dot(block, turn, preferred_element_type=jnp.float32)
    exchange(lambda i: i)

    for d in range(1, reach):
        gp.step(d)
    gq.start()
    gp.step(reach)
    for d in range(reach + 1):
        gp.wait_twin(d)

    keep(cross(*operand(lambda g: g), *branch(3), False), fbuf)
    exchange(lambda i: i)
    w4 = [turned_rows(w) for w in branch(4)]
    keep(cross(*operand(lambda g: order_ref[3, g]), *w4, False), sbuf)
    gq.step(1)
    w2 = [turned_rows(w) for w in branch(2)]
    keep(cross(*operand(lambda g: order_ref[4, undo(2, g)]), *w2, True), fbuf)
    exchange(lambda i: undo(1, i))
    gq.step(2)
    keep(cross(*operand(lambda g: g), *branch(1), True), fbuf)
    exchange(lambda i: i)
    w0 = [turned_cols(w) for w in branch(0)]
    last = cross(*operand(lambda g: undo(0, g)), *w0, True)
    for plane in (0, 1):
        for g in range(groups):
            part = last[plane][g * rows : (g + 1) * rows]
            dbuf[me, plane, :, pl.ds(g * width, width)] = part.astype(jnp.bfloat16)
    gd.start()
    gq.step(3)
    gq.step(reach)
    x_copy.wait()

    def join(origins, own=False):
        high = len(origins) * rows
        acc[...] = jnp.zeros_like(acc)

        @pl.loop(0, groups)
        def _(g):
            cols = pl.ds(pl.multiple_of(g * width, width), width)
            a = jnp.concatenate(
                [dbuf[o, plane, :, cols] for plane in (0, 1) for o in origins], axis=0
            )
            dims = (((1,), (1,)), ((), ()))
            for plane in (0, 1):
                acc[plane, : 2 * high] += lax.dot_general(
                    a, xbuf[plane, :, cols], dims, preferred_element_type=jnp.float32
                )

        for i, o in enumerate(origins):
            real = slice(i * rows, (i + 1) * rows)
            imag = slice(high + i * rows, high + (i + 1) * rows)
            near[turn_one, o, 0] = (acc[0, real] - acc[1, imag]).astype(near.dtype)
            near[turn_one, o, 1] = (acc[1, real] + acc[0, imag]).astype(near.dtype)
            if not (own and i == 0):
                trade(turn_one, o, o).start()

    turn_one, turn_two = 0, 1

    def trade(turn_at, target, slot):
        return pltpu.make_async_remote_copy(
            src_ref=near.at[turn_at, target], dst_ref=far.at[turn_at, me],
            send_sem=near_sems.at[turn_at, slot], recv_sem=far_sems.at[turn_at, me],
            device_id={"row": target}, device_id_type=pl.DeviceIdType.MESH,
        )

    def arrival(turn_at, source):
        return pltpu.make_async_remote_copy(
            src_ref=near.at[turn_at, source], dst_ref=far.at[turn_at, source],
            send_sem=near_sems.at[turn_at, source], recv_sem=far_sems.at[turn_at, source],
            device_id={"row": source}, device_id_type=pl.DeviceIdType.MESH,
        )

    def arrivals(turn_at):
        far[turn_at, me] = near[turn_at, me]

        @pl.loop(1, n)
        def _(i):
            arrival(turn_at, lax.rem(me + i, n)).wait_recv()

    gd.wait_twin(0)
    join([me, gd.twin], own=True)
    for d in range(1, reach):
        gd.step(d)
        if d == reach - 1:
            ge.start()
        gd.wait_twin(d)
        join([gd.origin(side, d, core) for side in (0, 1) for core in (0, 1)])
    for d in range(reach + 1):
        gq.wait_twin(d)

    def row_factor(s):
        buf, at = (qbuf, s) if s < early else (ebuf, s - early)
        return [buf[:, plane, at].reshape(width, width) for plane in (0, 1)]

    q1 = [turned_rows(w) for w in row_factor(0)]
    q5 = [turned_cols(w) for w in row_factor(2)]
    for plane in (0, 1):
        wbuf[0, plane] = q1[plane]
        wbuf[1, plane] = q5[plane]
    gd.step(reach)
    gd.wait_twin(reach)
    join([gd.origin(0, reach, core) for core in (0, 1)])
    ge.step(1)
    arrivals(turn_one)

    pieces = n // groups
    whole = [
        jnp.concatenate(
            [
                jnp.concatenate([far[turn_one, g * pieces + i, plane] for i in range(pieces)], axis=1)
                for g in range(groups)
            ],
            axis=0,
        )
        for plane in (0, 1)
    ]
    keep(cross(*whole, wbuf[0, 0], wbuf[0, 1], True), fbuf)
    exchange(lambda i: i)
    ge.step(2)
    keep(cross(*operand(lambda g: g), *row_factor(1), True), fbuf)
    exchange(lambda i: i)
    ge.step(3)
    mixed = cross(*operand(lambda g: g), wbuf[1, 0], wbuf[1, 1], True)
    tall = width // pieces
    for plane in (0, 1):
        for o in range(n):
            g, i = o // pieces, o % pieces
            block = mixed[plane][g * rows : (g + 1) * rows, i * tall : (i + 1) * tall]
            near[turn_two, o, plane] = block.astype(near.dtype)

    @pl.loop(1, n)
    def _(i):
        target = lax.rem(me + i, n)
        trade(turn_two, target, target).start()

    ge.step(reach)
    for d in range(reach + 1):
        ge.wait_twin(d)
    ends = cross(*row_factor(4), *row_factor(3), False)
    for plane in (0, 1):
        wbuf[2, plane] = ends[plane].astype(wbuf.dtype)
    arrivals(turn_two)

    amplitude = cross(
        *[far[turn_two, :, plane].reshape(width, tall).T for plane in (0, 1)],
        wbuf[2, 0], wbuf[2, 1], True,
    )
    for plane in (0, 1):
        out_ref[plane] = amplitude[plane]

    for turn_at in (turn_one, turn_two):

        @pl.loop(1, n)
        def _(i):
            arrival(turn_at, lax.rem(me + i, n)).wait_send()

    for gather in gathers:
        gather.finish()


def fused(n, left_stem, right_stem, branches, bits, order):
    planes, tall, cols = left_stem.shape
    rows = right_stem.shape[1]
    part, width = branches.shape[3:]
    sweeps, groups = order.shape
    vmem = pl.BlockSpec(memory_space=pltpu.VMEM)
    smem = pl.BlockSpec(memory_space=pltpu.SMEM)
    bf16 = jnp.bfloat16
    slots = 8 * (n // 4) + 2
    return pl.pallas_call(
        functools.partial(core_kernel, n),
        out_shape=jax.ShapeDtypeStruct((planes, tall, width), jnp.float32),
        in_specs=[pl.BlockSpec(memory_space=pl.ANY), vmem, vmem, smem, smem],
        out_specs=vmem,
        scratch_shapes=[
            pltpu.VMEM((n, planes, sweeps, part, width), bf16),
            pltpu.VMEM((n, planes, sweeps - 1, part, width), bf16),
            pltpu.VMEM((n, planes, rows, cols), bf16),
            pltpu.VMEM((n, planes, 1, part, width), bf16),
            pltpu.VMEM((planes, tall, cols), bf16),
            pltpu.VMEM((planes, groups, rows, width), jnp.float32),
            pltpu.VMEM((planes, groups, rows, width), bf16),
            pltpu.VMEM((planes, 8 * rows, tall), jnp.float32),
            pltpu.VMEM((2, n, planes, rows, tall), bf16),
            pltpu.VMEM((2, n, planes, rows, tall), bf16),
            pltpu.VMEM((3, planes, width, width), bf16),
            pltpu.SemaphoreType.DMA,
            pltpu.SemaphoreType.DMA((4, slots)),
            pltpu.SemaphoreType.DMA((4, slots)),
            pltpu.SemaphoreType.DMA((2, n)),
            pltpu.SemaphoreType.DMA((2, n)),
        ],
        compiler_params=pltpu.CompilerParams(
            collective_id=0, has_side_effects=True, vmem_limit_bytes=58 * 2**20
        ),
    )(left_stem, right_stem, branches, bits, order)


def fits(n, left_stem, right_stem, branches, order):
    part, width = branches.shape[3:]
    groups = order.shape[1]
    return (
        n % 8 == 0 and n // 4 == 4 and part % 16 == 0 and right_stem.shape[1] % 16 == 0
        and width // groups == 64 and n * left_stem.shape[1] == groups * width
        and n % groups == 0 and n * right_stem.shape[1] == width and order.shape[0] == 5
    )


def shards(n, left_stem, right_stem, branches, slice_bits, perms):
    left_sweeps = 3
    sweeps = perms.shape[0]

    scale = (2.0 * left_stem.shape[2]) ** (-0.5)
    if fits(n, left_stem, right_stem, branches, perms):
        return fused(n, left_stem, right_stem, branches, slice_bits, perms) * scale

    def own(index):
        return lax.dynamic_index_in_dim(branches[index], slice_bits[index], 0, keepdims=False)

    def fetch(indices):
        stacked = jnp.stack([own(index) for index in indices])
        return lax.all_gather(stacked, "row", axis=2, tiled=True)

    row_mats = fetch([2 * s + 1 for s in range(sweeps)])
    col_mats = fetch([2 * s for s in range(sweeps)])
    stem = right_stem
    for s in range(left_sweeps, sweeps):
        stem = permute(mix(stem, col_mats[s], s % 2 == 1, False), perms[s])
    for s in reversed(range(left_sweeps)):
        stem = permute(stem, jnp.argsort(perms[s]))
        stem = mix(stem, col_mats[s], s % 2 == 1, True)
    gathered = lax.all_gather(stem, "row", axis=1, tiled=True)
    joined = contract(gathered, left_stem, ((1,), (1,))).astype(jnp.bfloat16)

    spread = lax.all_to_all(joined, "row", split_axis=1, concat_axis=2, tiled=True)
    for s in range(left_sweeps):
        spread = mix(spread, row_mats[s], s % 2 == 1, True)
    turned = lax.all_to_all(spread, "row", split_axis=2, concat_axis=1, tiled=True)

    right_rows = row_mats[left_sweeps]
    for s in range(left_sweeps + 1, sweeps):
        right_rows = contract(row_mats[s], right_rows, ((1,), (0,))).astype(jnp.bfloat16)
    return contract(turned, right_rows, ((0,), (1,))) * scale


def solution(mesh):
    in_specs = (
        P(None, ("cuts", "row"), None),
        P(None, ("cuts", "row"), None),
        P(None, None, None, "row", None),
        P("cuts"),
        P("cuts", None),
    )
    out_specs = P(None, ("cuts", "row"), None)
    return jax.shard_map(functools.partial(shards, mesh.shape["row"]), mesh=mesh, in_specs=in_specs, out_specs=out_specs, check_vma=False)
```
